512 devices in a mesh: dp: 32 (over z_hi, y, core), seq: 16 (over z_lo, x).
Axes of the slice: x: 4, y: 4, z: 16 (z_hi: 4, z_lo: 4; z = z_hi * 4 + z_lo), core: 2. Of those that a mesh axis runs over, the one named last changes fastest.
Arguments:
- cond_vec: float32 [32, 3072], P('dp', 'seq'), may hold values from -6 to 6
- mod_weight: bfloat16 [2, 3072, 3072], P(None, 'seq', 'dp'), may hold values from -0.109375 to 0.109375
- text_hidden: bfloat16 [32, 512, 3072], P('dp', 'seq'), may hold values from -121 to 121
- text_grad: bfloat16 [32, 512, 3072], P('dp', 'seq'), may hold values from -14 to 14, as said below
- queries: bfloat16 [32, 2048, 2048], P('dp', 'seq'), may hold values from -4.5 to 4.5
- keys: bfloat16 [32, 2048, 2048], P('dp', 'seq'), may hold values from -4.5 to 4.5
- values: bfloat16 [32, 2048, 2048], P('dp', 'seq'), may hold values from -6 to 6
- out_grad: bfloat16 [32, 2048, 2048], P('dp', 'seq'), may hold values from -6 to 6
Outputs:
- text_hidden_grad: bfloat16 [32, 512, 3072], P('dp', 'seq')
- mod_weight_grad: float32 [2, 3072, 3072], P(None, 'seq', 'dp')
- cond_vec_grad: float32 [32, 3072], P('dp', 'seq')
- query_grad: bfloat16 [32, 2048, 2048], P('dp', 'seq')
- key_grad: bfloat16 [32, 2048, 2048], P('dp', 'seq')
- value_grad: bfloat16 [32, 2048, 2048], P('dp', 'seq')
The draws below stay inside these ranges and needn't reach their ends.
Inputs may be any that keep to these rules, and one draw needn't show every extreme that they name: `text_grad`: incoming gradient.
All inputs are finite; a program needn't handle non-finite values.
Results may differ from the reference program's by a relative error of at most 0.0087.
Values may be sent and summed in bfloat16 or wider, within the bound.
A program may use at most 64 MiB of HBM per device.

```python
import jax
import jax.numpy as jnp
from jax import lax

D = 3072
HEADS = 16
HEAD_DIM = 128
TXT = 512
JOINT = 2048
BATCH = 32


def drawn_pair(key):
    base = jax.random.fold_in(key, 7)
    first, second = jax.random.split(base, 2)
    width = HEADS * HEAD_DIM
    query = jnp.clip(jax.random.normal(first, (BATCH, JOINT, width), jnp.float32), -4.5, 4.5)
    key_rows = jnp.clip(jax.random.normal(second, (BATCH, JOINT, width), jnp.float32), -4.5, 4.5)
    return (query, key_rows)


def draw_queries(key, part):
    return drawn_pair(key)[0].astype(jnp.bfloat16)


def draw_keys(key, part):
    return drawn_pair(key)[1].astype(jnp.bfloat16)


def draw_text_hidden(key, part):
    first = jax.random.fold_in(jax.random.fold_in(key, 11), 0)
    values_drawn = jnp.clip(jax.random.normal(first, (BATCH, TXT, D), jnp.float32), -6.0, 6.0)
    return values_drawn.astype(jnp.bfloat16)


def draw_text_grad(key, part):
    first = jax.random.fold_in(jax.random.fold_in(key, 13), 0)
    rising = 1.0 + 2.0 * jnp.arange(TXT, dtype=jnp.float32) / (TXT - 1)
    values_drawn = 0.5 * jnp.clip(jax.random.normal(first, (BATCH, TXT, D), jnp.float32), -6.0, 6.0)
    values_drawn = values_drawn * rising[None, :, None]
    return values_drawn.astype(jnp.bfloat16)


def steps_of(rng, shape, pieces, smallest, top_value):
    gain, own = 1.0, jax.random.fold_in(rng, 6)
    for axis_at, shards_of in pieces:
        steps = jnp.exp(jax.random.uniform(jax.random.fold_in(own, axis_at), (shards_of,), jnp.float32, smallest / len(pieces), top_value / len(pieces)))
        gain = gain * jnp.repeat(steps, shape[axis_at] // shards_of).reshape([-1 if axis == axis_at else 1 for axis in range(len(shape))])
    return gain


def normal_values(key, extent, scale, reach, shards=(), kind=jnp.bfloat16):
    level = steps_of(key, extent, shards, -0.22, 0.18) if shards else 1.0
    drawn = jax.random.normal(key, extent, jnp.float32) * scale * level
    return jnp.minimum(jnp.maximum(drawn, -reach), reach).astype(kind)


def setup_inputs(seed: int = 0) -> dict:
    splits = jax.random.split(jax.random.key(seed), 9)
    cond_vec = normal_values(splits[0], (BATCH, D), 1.0, 6.0, ((0, 32), (1, 16)), jnp.float32)
    mod_weight = normal_values(splits[1], (2, D, D), D ** -0.5, 0.109375, ((1, 16), (2, 32)))
    text_hidden = draw_text_hidden(jax.random.fold_in(splits[8], 71), 0)
    text_grad = draw_text_grad(jax.random.fold_in(splits[8], 71), 0)
    queries = draw_queries(jax.random.fold_in(splits[8], 71), 0)
    keys = draw_keys(jax.random.fold_in(splits[8], 71), 0)
    values = normal_values(splits[6], (BATCH, JOINT, HEADS * HEAD_DIM), 1.0, 6.0, ((0, 32), (1, 16)))
    out_grad = normal_values(splits[7], (BATCH, JOINT, HEADS * HEAD_DIM), 1.0, 6.0, ((0, 32), (1, 16)))
    return {"cond_vec": cond_vec, "mod_weight": mod_weight, "text_hidden": text_hidden, "text_grad": text_grad, "queries": queries, "keys": keys, "values": values, "out_grad": out_grad}


norm_eps = 1e-06

def attend_head(arrays):
    query, key_rows, value, grad_out = arrays
    factor = query.shape[-1] ** (-0.5)
    qf = query.astype(jnp.float32)
    kf = key_rows.astype(jnp.float32)
    vf = value.astype(jnp.float32)
    gf = grad_out.astype(jnp.float32)
    scores = jnp.einsum('sd,td->st', qf, kf) * factor
    peak = lax.optimization_barrier(jnp.max(scores, axis=-1, keepdims=True))
    exponent = jnp.exp(scores - peak)
    probability = exponent / lax.optimization_barrier(jnp.sum(exponent, axis=-1, keepdims=True))
    prob_low = lax.optimization_barrier(probability.astype(jnp.bfloat16)).astype(jnp.float32)
    attn_out = jnp.einsum('st,td->sd', prob_low, vf)
    row_delta = lax.optimization_barrier(jnp.sum(gf * attn_out, axis=-1, keepdims=True))
    value_grad = jnp.einsum('st,sd->td', prob_low, gf).astype(jnp.bfloat16)
    prob_grad = jnp.einsum('sd,td->st', gf, vf)
    score_grad = probability * (prob_grad - row_delta) * factor
    score_low = lax.optimization_barrier(score_grad.astype(jnp.bfloat16)).astype(jnp.float32)
    query_grad = jnp.einsum('st,td->sd', score_low, kf).astype(jnp.bfloat16)
    key_grad = jnp.einsum('st,sd->td', score_low, qf).astype(jnp.bfloat16)
    return (query_grad, key_grad, value_grad)

def per_sample(arrays):
    shaped = tuple((a.reshape(JOINT, HEADS, HEAD_DIM).transpose(1, 0, 2) for a in arrays))
    grads = lax.map(attend_head, shaped)
    return tuple((g.transpose(1, 0, 2).reshape(JOINT, HEADS * HEAD_DIM) for g in grads))

def reference(cond_vec, mod_weight, text_hidden, text_grad, queries, keys, values, out_grad):
    act = jax.nn.silu(cond_vec).astype(jnp.bfloat16)
    mod_scale = jnp.dot(act, mod_weight[1], preferred_element_type=jnp.float32)
    hidden = text_hidden.astype(jnp.float32)
    incoming = text_grad.astype(jnp.float32)
    centred = hidden - lax.optimization_barrier(jnp.mean(hidden, axis=-1, keepdims=True))
    inv_std = lax.rsqrt(lax.optimization_barrier(jnp.mean(centred * centred, axis=-1, keepdims=True)) + norm_eps)
    normed = centred * inv_std
    grad_mod = jnp.stack([lax.optimization_barrier(jnp.sum(incoming, axis=1)), lax.optimization_barrier(jnp.sum(incoming * normed, axis=1))], axis=1)
    upstream = incoming * (1.0 + mod_scale[:, None, :])
    text_hidden_grad = inv_std * (upstream - lax.optimization_barrier(jnp.mean(upstream, axis=-1, keepdims=True)) - normed * lax.optimization_barrier(jnp.mean(upstream * normed, axis=-1, keepdims=True)))
    text_hidden_grad = text_hidden_grad.astype(jnp.bfloat16)
    act_wide = act.astype(jnp.float32)
    mod_weight_grad = jnp.einsum('br,bkc->krc', act_wide, grad_mod, precision=lax.Precision.HIGHEST)
    weight_wide = mod_weight.astype(jnp.float32)
    backward = jnp.einsum('bkc,krc->br', grad_mod, weight_wide, precision=lax.Precision.HIGHEST)
    sigma = jax.nn.sigmoid(cond_vec)
    cond_vec_grad = backward * sigma * (1.0 + cond_vec * (1.0 - sigma))
    query_grad, key_grad, value_grad = lax.map(per_sample, (queries, keys, values, out_grad))
    return (text_hidden_grad, mod_weight_grad, cond_vec_grad, query_grad, key_grad, value_grad)
```

```python
import math

import jax
import jax.numpy as jnp
from jax import lax
from jax.experimental import pallas as pl
from jax.experimental.pallas import tpu as pltpu
from jax.sharding import PartitionSpec as P

HEADS = 16
HEAD_DIM = 128
NORM_EPS = 1e-06
PEERS = 16
BLOCK = 4
CHUNK = 256
LOG2E = math.log2(math.e)
MESH = pl.DeviceIdType.MESH


def place_to(me, s):
    return ((me // 4 + s % 4) % 4) * 4 + (me % 4 + s // 4) % 4


def place_from(me, s):
    return ((me // 4 + 4 - s % 4) % 4) * 4 + (me % 4 + 4 - s // 4) % 4


def nt(a, b):
    return lax.dot_general(a, b, (((1,), (1,)), ((), ())), preferred_element_type=jnp.float32)


def nn(a, b):
    return lax.dot_general(a, b, (((1,), (0,)), ((), ())), preferred_element_type=jnp.float32)


def attention_kernel(
    q_ref, k_ref, v_ref, g_ref, dq_ref, dk_ref, dv_ref,
    qb, kb, vb, gb, kt, u, dp, dka, dva, dqo, dko, dvo, send, recv, local,
):
    rows = q_ref.shape[0]
    width = qb.shape[2]
    tokens = PEERS * rows
    chunks = tokens // CHUNK
    block = BLOCK * rows
    factor = width ** (-0.5)
    me = lax.axis_index("seq")

    def head_of(device):
        return pl.ds(pl.multiple_of(device * width, width), width)

    ins = ((k_ref, kb), (v_ref, vb), (q_ref, qb), (g_ref, gb))
    outs = ((dqo, dq_ref), (dko, dk_ref), (dvo, dv_ref))

    def inward(a, s):
        src, dst = ins[a]
        to = place_to(me, s)
        return pltpu.make_async_remote_copy(
            src.at[:, head_of(to)], dst.at[s], send.at[a, s], recv.at[a, s],
            device_id={"seq": to}, device_id_type=MESH,
        )

    def outward(a, s):
        src, dst = outs[a]
        return pltpu.make_async_remote_copy(
            src.at[s], dst.at[:, head_of(me)], send.at[4 + a, s], recv.at[4 + a, s],
            device_id={"seq": place_from(me, s)}, device_id_type=MESH,
        )

    def own_in(a):
        src, dst = ins[a]
        return pltpu.make_async_copy(src.at[:, head_of(me)], dst.at[0], local.at[a])

    def own_out(a):
        src, dst = outs[a]
        return pltpu.make_async_copy(src.at[0], dst.at[:, head_of(me)], local.at[4 + a])

    for a in range(4):
        own_in(a).start()

    barrier = pltpu.get_barrier_semaphore()

    @pl.loop(1, PEERS)
    def _(s):
        pl.semaphore_signal(
            barrier, inc=1, device_id={"seq": place_to(me, s)}, device_id_type=MESH
        )

    pl.semaphore_wait(barrier, PEERS - 1)

    for group in ((0,), (1,), (2, 3)):

        @pl.loop(1, PEERS)
        def _(s):
            for a in group:
                inward(a, s).start()

    dka[...] = jnp.zeros_like(dka)
    dva[...] = jnp.zeros_like(dva)
    for a in range(4):
        own_in(a).wait()

    @pl.loop(1, PEERS)
    def _(s):
        inward(0, s).wait_recv()

    for s in range(PEERS):
        kt[:, s * rows : (s + 1) * rows] = kb[s].astype(jnp.float32).T.astype(jnp.bfloat16)

    @pl.loop(1, PEERS)
    def _(s):
        inward(1, s).wait_recv()

    per_chunk = CHUNK // rows

    @pl.loop(0, PEERS // BLOCK)
    def _(i):
        first = i * BLOCK
        for j in range(BLOCK):

            @pl.when(first + j > 0)
            def _():
                inward(2, first + j).wait_recv()
                inward(3, first + j).wait_recv()

        here = pl.ds(pl.multiple_of(first, BLOCK), BLOCK)
        queries = qb[here].reshape(block, width)
        grads = gb[here].reshape(block, width)
        peak = None
        for t in range(chunks):
            keys = kb[t * per_chunk : (t + 1) * per_chunk].reshape(CHUNK, width)
            scores = nt(keys, queries)
            u[t] = scores
            top = jnp.max(scores.reshape(CHUNK // 8, 8, block), axis=0)
            peak = top if peak is None else jnp.maximum(peak, top)
        peak = jnp.max(peak, axis=0, keepdims=True)
        total = jnp.zeros((8, block), jnp.float32)
        delta = jnp.zeros((8, block), jnp.float32)
        for t in range(chunks):
            values = vb[t * per_chunk : (t + 1) * per_chunk].reshape(CHUNK, width)
            prob_grad = nt(values, grads)
            exponent = jnp.exp2((u[t] - peak) * (factor * LOG2E))
            total += jnp.sum(exponent.reshape(CHUNK // 8, 8, block), axis=0)
            delta += jnp.sum((exponent * prob_grad).reshape(CHUNK // 8, 8, block), axis=0)
            u[t] = exponent
            dp[t] = prob_grad
        inverse = 1.0 / jnp.sum(total, axis=0, keepdims=True)
        delta = jnp.sum(delta, axis=0, keepdims=True) * inverse
        query_grad = jnp.zeros((width, block), jnp.float32)
        for t in range(chunks):
            at = slice(t * CHUNK, (t + 1) * CHUNK)
            probability = u[t] * inverse
            score_low = (probability * (dp[t] - delta)).astype(jnp.bfloat16)
            dva[at] += nn(probability.astype(jnp.bfloat16), grads)
            dka[at] += nn(score_low, queries)
            query_grad += nn(kt[:, at], score_low)
        dqo[here] = (
            (query_grad * factor).T.astype(jnp.bfloat16).reshape(BLOCK, rows, width)
        )
        for j in range(BLOCK):

            @pl.when(first + j > 0)
            def _():
                outward(0, first + j).start()

    own_out(0).start()
    for s in range(PEERS):
        at = slice(s * rows, (s + 1) * rows)
        dko[s] = (dka[at] * factor).astype(jnp.bfloat16)
        dvo[s] = dva[at].astype(jnp.bfloat16)

    @pl.loop(1, PEERS)
    def _(s):
        outward(1, s).start()
        outward(2, s).start()

    own_out(1).start()
    own_out(2).start()

    @pl.loop(1, PEERS)
    def _(s):
        for a in range(4):
            inward(a, s).wait_send()
        for a in range(3):
            outward(a, s).wait_send()

    for a in range(3):
        own_out(a).wait()

    @pl.loop(1, PEERS)
    def _(s):
        for a in range(3):
            outward(a, s).wait_recv()


def attention(q, k, v, g):
    rows, width = q.shape
    slots = pltpu.VMEM((PEERS, rows, HEAD_DIM), jnp.bfloat16)
    tokens = PEERS * rows
    scores = pltpu.VMEM((tokens // CHUNK, CHUNK, BLOCK * rows), jnp.float32)
    total = pltpu.VMEM((tokens, HEAD_DIM), jnp.float32)
    anywhere = pl.BlockSpec(memory_space=pl.ANY)
    return pl.pallas_call(
        attention_kernel,
        out_shape=[jax.ShapeDtypeStruct((rows, width), jnp.bfloat16)] * 3,
        in_specs=[anywhere] * 4,
        out_specs=[anywhere] * 3,
        scratch_shapes=[
            slots, slots, slots, slots,
            pltpu.VMEM((HEAD_DIM, tokens), jnp.bfloat16),
            scores, scores, total, total,
            slots, slots, slots,
            pltpu.SemaphoreType.DMA((7, PEERS)),
            pltpu.SemaphoreType.DMA((7, PEERS)),
            pltpu.SemaphoreType.DMA((7,)),
        ],
        compiler_params=pltpu.CompilerParams(
            collective_id=0, has_side_effects=True, vmem_limit_bytes=50 * 2**20
        ),
        cost_estimate=pl.CostEstimate(
            flops=10 * tokens * tokens * HEAD_DIM,
            bytes_accessed=14 * rows * width,
            transcendentals=tokens * tokens,
        ),
    )(q, k, v, g)


def from_everyone(x, axis):
    copies = jnp.broadcast_to(x, (lax.axis_size(axis), *x.shape))
    return lax.all_to_all(copies, axis, split_axis=0, concat_axis=0, tiled=True)


def split_up(x, dim, devices):
    shape = x.shape
    tiles = x.reshape(*shape[:dim], devices, shape[dim] // devices, *shape[dim + 1 :])
    return jnp.moveaxis(tiles, dim, 0)


def per_device(cond_vec, mod_weight, text_hidden, text_grad, queries, keys, values, out_grad):
    query_grad, key_grad, value_grad = attention(queries[0], keys[0], values[0], out_grad[0])
    cond_all = from_everyone(cond_vec, "dp")[:, 0]
    act = jax.nn.silu(cond_all).astype(jnp.bfloat16)
    partial_scale = jnp.dot(act, mod_weight[1], preferred_element_type=jnp.float32)
    summed_scale = jnp.sum(from_everyone(partial_scale, "seq"), axis=0)
    mod_scale = lax.all_to_all(summed_scale, "dp", split_axis=0, concat_axis=1, tiled=True)
    hidden = text_hidden.astype(jnp.float32)
    incoming = text_grad.astype(jnp.float32)
    centred = hidden - jnp.mean(hidden, axis=-1, keepdims=True)
    inv_std = lax.rsqrt(jnp.mean(centred * centred, axis=-1, keepdims=True) + NORM_EPS)
    normed = centred * inv_std
    grad_mod = jnp.stack([jnp.sum(incoming, axis=1), jnp.sum(incoming * normed, axis=1)], axis=1)
    upstream = incoming * (1.0 + mod_scale[:, None, :])
    text_hidden_grad = inv_std * (
        upstream
        - jnp.mean(upstream, axis=-1, keepdims=True)
        - normed * jnp.mean(upstream * normed, axis=-1, keepdims=True)
    )
    text_hidden_grad = text_hidden_grad.astype(jnp.bfloat16)
    summed_grad = jnp.sum(from_everyone(grad_mod, "seq"), axis=0)
    tiles = split_up(summed_grad, 2, lax.axis_size("dp"))
    owner_grad = lax.all_to_all(tiles, "dp", split_axis=0, concat_axis=0, tiled=True)[:, 0]
    mod_weight_grad = jnp.einsum(
        "br,bkc->krc", act.astype(jnp.float32), owner_grad, precision=lax.Precision.HIGHEST
    )
    backward = jnp.einsum(
        "bkc,krc->br", owner_grad, mod_weight.astype(jnp.float32), precision=lax.Precision.HIGHEST
    )
    arrived = lax.all_to_all(backward, "dp", split_axis=0, concat_axis=0, tiled=True)
    summed_back = arrived.sum(axis=0, keepdims=True)
    sigma = jax.nn.sigmoid(cond_vec)
    cond_vec_grad = summed_back * sigma * (1.0 + cond_vec * (1.0 - sigma))
    return (
        text_hidden_grad, mod_weight_grad, cond_vec_grad,
        query_grad[None], key_grad[None], value_grad[None],
    )


def solution(mesh):
    tokens = P("dp", "seq", None)
    weights = P(None, "seq", "dp")
    return jax.shard_map(
        per_device,
        mesh=mesh,
        in_specs=(P("dp", "seq"), weights, tokens, tokens, tokens, tokens, tokens, tokens),
        out_specs=(tokens, weights, P("dp", "seq"), tokens, tokens, tokens),
        check_vma=False,
    )
```

```python
import math

import jax
import jax.numpy as jnp
from jax import lax
from jax.experimental import pallas as pl
from jax.experimental.pallas import tpu as pltpu
from jax.sharding import PartitionSpec as P

HEADS = 16
HEAD_DIM = 128
NORM_EPS = 1e-06
PEERS = 16
SAMPLES = 32
LANES = 128
BLOCK = 4
CHUNK = 256
LOG2E = math.log2(math.e)
MESH = pl.DeviceIdType.MESH


def place_to(me, s):
    return ((me // 4 + s % 4) % 4) * 4 + (me % 4 + s // 4) % 4


def place_from(me, s):
    return ((me // 4 + 4 - s % 4) % 4) * 4 + (me % 4 + 4 - s // 4) % 4


def nt(a, b):
    return lax.dot_general(a, b, (((1,), (1,)), ((), ())), preferred_element_type=jnp.float32)


def nn(a, b):
    return lax.dot_general(a, b, (((1,), (0,)), ((), ())), preferred_element_type=jnp.float32)


def joint_kernel(
    cond_ref, weight_ref, hidden_ref, incoming_ref, q_ref, k_ref, v_ref, g_ref,
    hidden_grad_ref, weight_grad_ref, cond_grad_ref, dq_ref, dk_ref, dv_ref,
    qb, kb, vb, gb, kt, u, dp, dka, dva, dqo, dko, dvo,
    cond_own, cond_all, parcel, parcels, partial, share, whole, back, backs, row, normed, spread,
    send, recv, local, dp_send, dp_recv, seq_send, seq_recv,
):
    rows = q_ref.shape[0]
    width = qb.shape[2]
    tokens = PEERS * rows
    chunks = tokens // CHUNK
    block = BLOCK * rows
    factor = width ** (-0.5)
    me = lax.axis_index("seq")
    mine = lax.axis_index("dp")
    weight_rows, columns = weight_ref.shape[1:]
    features = hidden_ref.shape[1]
    text_rows = hidden_ref.shape[0]

    def head_of(device):
        return pl.ds(pl.multiple_of(device * width, width), width)

    ins = ((k_ref, kb), (v_ref, vb), (q_ref, qb), (g_ref, gb))
    outs = ((dqo, dq_ref), (dko, dk_ref), (dvo, dv_ref))

    def inward(a, s):
        src, dst = ins[a]
        to = place_to(me, s)
        return pltpu.make_async_remote_copy(
            src.at[:, head_of(to)], dst.at[s], send.at[a, s], recv.at[a, s],
            device_id={"seq": to}, device_id_type=MESH,
        )

    def outward(a, s):
        src, dst = outs[a]
        return pltpu.make_async_remote_copy(
            src.at[s], dst.at[:, head_of(me)], send.at[4 + a, s], recv.at[4 + a, s],
            device_id={"seq": place_from(me, s)}, device_id_type=MESH,
        )

    def own_in(a):
        src, dst = ins[a]
        return pltpu.make_async_copy(src.at[:, head_of(me)], dst.at[0], local.at[a])

    def own_out(a):
        src, dst = outs[a]
        return pltpu.make_async_copy(src.at[0], dst.at[:, head_of(me)], local.at[4 + a])

    def other(r):
        return (mine + r) % SAMPLES

    def dp_copy(step, r, arriving):
        src = (cond_own, parcel.at[other(r)], back.at[other(r)])[step]
        dst = (cond_all, parcels, backs)[step]
        place = other(r) if arriving else mine
        return pltpu.make_async_remote_copy(
            src, dst.at[place], dp_send.at[step, r], dp_recv.at[step, place],
            device_id={"dp": other(r)}, device_id_type=MESH,
        )

    def scatter_copy(s):
        to = place_to(me, s)
        return pltpu.make_async_remote_copy(
            parcels.at[pl.ds(to * 2, 2)], partial.at[s], seq_send.at[0, s], seq_recv.at[0, s],
            device_id={"seq": to}, device_id_type=MESH,
        )

    def gather_copy(s, arriving):
        place = place_from(me, s) if arriving else me
        return pltpu.make_async_remote_copy(
            share, whole.at[pl.ds(place * 2, 2)], seq_send.at[1, s], seq_recv.at[1, s],
            device_id={"seq": place_to(me, s)}, device_id_type=MESH,
        )

    def each(low, high, action):
        pl.loop(low, high)(action)

    cond_own[...] = jnp.zeros_like(cond_own)
    cond_own[:, :weight_rows] = cond_ref[...]
    for a in range(4):
        own_in(a).start()

    barrier = pltpu.get_barrier_semaphore()

    @pl.loop(1, SAMPLES)
    def _(r):
        pl.semaphore_signal(barrier, inc=1, device_id={"dp": other(r)}, device_id_type=MESH)

    @pl.loop(1, PEERS)
    def _(s):
        pl.semaphore_signal(
            barrier, inc=1, device_id={"seq": place_to(me, s)}, device_id_type=MESH
        )

    pl.semaphore_wait(barrier, PEERS + SAMPLES - 2)

    each(1, SAMPLES, lambda r: dp_copy(0, r, False).start())
    each(1, PEERS, lambda s: inward(0, s).start())
    each(1, PEERS, lambda s: inward(1, s).start())

    plain = jnp.zeros((8, features), jnp.float32)
    scaled = jnp.zeros((8, features), jnp.float32)
    for t in range(0, text_rows, 16):
        at = slice(t, t + 16)
        hidden = hidden_ref[at].astype(jnp.float32)
        incoming = incoming_ref[at].astype(jnp.float32)
        centred = hidden - jnp.sum(hidden, axis=-1, keepdims=True) * (1.0 / features)
        variance = jnp.sum(centred * centred, axis=-1, keepdims=True) * (1.0 / features)
        inv_std = lax.rsqrt(variance + NORM_EPS)
        norm = centred * inv_std
        normed[at] = norm
        spread[at] = jnp.broadcast_to(inv_std, (16, LANES))
        plain += jnp.sum(incoming.reshape(2, 8, features), axis=0)
        scaled += jnp.sum((incoming * norm).reshape(2, 8, features), axis=0)
    plain = jnp.sum(plain, axis=0, keepdims=True)
    scaled = jnp.sum(scaled, axis=0, keepdims=True)
    parcel[...] = jnp.zeros_like(parcel)
    back[...] = jnp.zeros_like(back)
    for p in range(SAMPLES):
        at = slice(p * columns, (p + 1) * columns)
        parcel[p, :, LANES : LANES + columns] = plain[:, at]
        parcel[p, :, 2 * LANES : 2 * LANES + columns] = scaled[:, at]

    cond_all[mine] = cond_own[...]
    each(1, SAMPLES, lambda r: dp_copy(0, r, True).wait_recv())
    cond = cond_all[...].reshape(SAMPLES, cond_all.shape[2])[:, :weight_rows]
    act = (cond * jax.nn.sigmoid(cond)).astype(jnp.bfloat16)
    parcel[:, :, :columns] = nn(act, weight_ref[1]).reshape(SAMPLES, 1, columns)
    each(1, SAMPLES, lambda r: dp_copy(1, r, False).start())

    @pl.loop(1, PEERS)
    def _(s):
        inward(2, s).start()
        inward(3, s).start()

    def scatter_sums():
        parcels[mine] = parcel[mine]
        each(1, SAMPLES, lambda r: dp_copy(1, r, True).wait_recv())
        each(1, PEERS, lambda s: scatter_copy(s).start())

    def gather_sums():
        partial[0] = parcels[pl.ds(me * 2, 2)]
        each(1, PEERS, lambda s: scatter_copy(s).wait_recv())
        share[...] = jnp.sum(partial[...], axis=0)
        each(1, PEERS, lambda s: gather_copy(s, False).start())

    def weight_gradients():
        whole[pl.ds(me * 2, 2)] = share[...]
        each(1, PEERS, lambda s: gather_copy(s, True).wait_recv())
        sums = whole[...].reshape(SAMPLES, whole.shape[2])
        cond = cond_all[...].reshape(SAMPLES, cond_all.shape[2])[:, :weight_rows]
        act = (cond * jax.nn.sigmoid(cond)).astype(jnp.bfloat16).astype(jnp.float32)
        backward = jnp.zeros((SAMPLES, weight_rows), jnp.float32)
        for k in range(2):
            grad = sums[:, (k + 1) * LANES : (k + 1) * LANES + columns]
            weight_grad_ref[k] = lax.dot_general(
                act, grad, (((0,), (0,)), ((), ())),
                precision=lax.Precision.HIGHEST, preferred_element_type=jnp.float32,
            )
            backward += lax.dot_general(
                grad, weight_ref[k].astype(jnp.float32), (((1,), (1,)), ((), ())),
                precision=lax.Precision.HIGHEST, preferred_element_type=jnp.float32,
            )
        back[:, :, :weight_rows] = backward.reshape(SAMPLES, 1, weight_rows)
        each(1, SAMPLES, lambda r: dp_copy(2, r, False).start())

    def text_gradient():
        for j in range(SAMPLES):
            row[:, j * columns : (j + 1) * columns] = whole[j, :, :columns]
        gain = 1.0 + row[...]
        for t in range(0, text_rows, 16):
            at = slice(t, t + 16)
            norm = normed[at]
            upstream = incoming_ref[at].astype(jnp.float32) * gain
            mean = jnp.sum(upstream, axis=-1, keepdims=True) * (1.0 / features)
            along = jnp.sum(upstream * norm, axis=-1, keepdims=True) * (1.0 / features)
            grad = spread[at, :1] * (upstream - mean - norm * along)
            hidden_grad_ref[at] = grad.astype(jnp.bfloat16)

    def cond_gradient():
        backs[mine] = back[mine]
        each(1, SAMPLES, lambda r: dp_copy(2, r, True).wait_recv())
        summed = jnp.sum(backs[...], axis=0)[:, :weight_rows]
        cond = cond_ref[...]
        sigma = jax.nn.sigmoid(cond)
        cond_grad_ref[...] = summed * sigma * (1.0 + cond * (1.0 - sigma))

    dka[...] = jnp.zeros_like(dka)
    dva[...] = jnp.zeros_like(dva)
    for a in range(4):
        own_in(a).wait()
    each(1, PEERS, lambda s: inward(0, s).wait_recv())

    for s in range(PEERS):
        kt[:, s * rows : (s + 1) * rows] = kb[s].astype(jnp.float32).T.astype(jnp.bfloat16)

    each(1, PEERS, lambda s: inward(1, s).wait_recv())

    per_chunk = CHUNK // rows

    @pl.loop(0, PEERS // BLOCK)
    def _(i):
        first = i * BLOCK
        for j in range(BLOCK):

            @pl.when(first + j > 0)
            def _():
                inward(2, first + j).wait_recv()
                inward(3, first + j).wait_recv()

        here = pl.ds(pl.multiple_of(first, BLOCK), BLOCK)
        queries = qb[here].reshape(block, width)
        grads = gb[here].reshape(block, width)
        peak = None
        for t in range(chunks):
            keys = kb[t * per_chunk : (t + 1) * per_chunk].reshape(CHUNK, width)
            scores = nt(keys, queries)
            u[t] = scores
            top = jnp.max(scores.reshape(CHUNK // 8, 8, block), axis=0)
            peak = top if peak is None else jnp.maximum(peak, top)
        peak = jnp.max(peak, axis=0, keepdims=True)
        total = jnp.zeros((8, block), jnp.float32)
        delta = jnp.zeros((8, block), jnp.float32)
        for t in range(chunks):
            values = vb[t * per_chunk : (t + 1) * per_chunk].reshape(CHUNK, width)
            prob_grad = nt(values, grads)
            exponent = jnp.exp2((u[t] - peak) * (factor * LOG2E))
            total += jnp.sum(exponent.reshape(CHUNK // 8, 8, block), axis=0)
            delta += jnp.sum((exponent * prob_grad).reshape(CHUNK // 8, 8, block), axis=0)
            u[t] = exponent
            dp[t] = prob_grad
        inverse = 1.0 / jnp.sum(total, axis=0, keepdims=True)
        delta = jnp.sum(delta, axis=0, keepdims=True) * inverse
        query_grad = jnp.zeros((width, block), jnp.float32)
        for t in range(chunks):
            at = slice(t * CHUNK, (t + 1) * CHUNK)
            probability = u[t] * inverse
            score_low = (probability * (dp[t] - delta)).astype(jnp.bfloat16)
            dva[at] += nn(probability.astype(jnp.bfloat16), grads)
            dka[at] += nn(score_low, queries)
            query_grad += nn(kt[:, at], score_low)
        dqo[here] = (
            (query_grad * factor).T.astype(jnp.bfloat16).reshape(BLOCK, rows, width)
        )
        for j in range(BLOCK):

            @pl.when(first + j > 0)
            def _():
                outward(0, first + j).start()

        pl.when(i == 0)(scatter_sums)
        pl.when(i == 1)(gather_sums)
        pl.when(i == 2)(weight_gradients)

    own_out(0).start()
    for s in range(PEERS):
        at = slice(s * rows, (s + 1) * rows)
        dko[s] = (dka[at] * factor).astype(jnp.bfloat16)
        dvo[s] = dva[at].astype(jnp.bfloat16)

    @pl.loop(1, PEERS)
    def _(s):
        outward(1, s).start()
        outward(2, s).start()

    own_out(1).start()
    own_out(2).start()
    text_gradient()
    cond_gradient()

    @pl.loop(1, SAMPLES)
    def _(r):
        for step in range(3):
            dp_copy(step, r, False).wait_send()

    @pl.loop(1, PEERS)
    def _(s):
        scatter_copy(s).wait_send()
        gather_copy(s, False).wait_send()

    @pl.loop(1, PEERS)
    def _(s):
        for a in range(4):
            inward(a, s).wait_send()
        for a in range(3):
            outward(a, s).wait_send()

    for a in range(3):
        own_out(a).wait()

    @pl.loop(1, PEERS)
    def _(s):
        for a in range(3):
            outward(a, s).wait_recv()


def joint(cond, weight, hidden, incoming, q, k, v, g):
    rows, width = q.shape
    slots = pltpu.VMEM((PEERS, rows, HEAD_DIM), jnp.bfloat16)
    tokens = PEERS * rows
    scores = pltpu.VMEM((tokens // CHUNK, CHUNK, BLOCK * rows), jnp.float32)
    total = pltpu.VMEM((tokens, HEAD_DIM), jnp.float32)
    anywhere = pl.BlockSpec(memory_space=pl.ANY)
    inside = pl.BlockSpec(memory_space=pltpu.VMEM)
    padded = -(-cond.shape[1] // LANES) * LANES
    f32 = jnp.float32
    return pl.pallas_call(
        joint_kernel,
        out_shape=[
            jax.ShapeDtypeStruct(hidden.shape, jnp.bfloat16),
            jax.ShapeDtypeStruct(weight.shape, f32),
            jax.ShapeDtypeStruct(cond.shape, f32),
        ]
        + [jax.ShapeDtypeStruct((rows, width), jnp.bfloat16)] * 3,
        in_specs=[inside] * 4 + [anywhere] * 4,
        out_specs=[inside] * 3 + [anywhere] * 3,
        scratch_shapes=[
            slots, slots, slots, slots,
            pltpu.VMEM((HEAD_DIM, tokens), jnp.bfloat16),
            scores, scores, total, total,
            slots, slots, slots,
            pltpu.VMEM((1, padded), f32),
            pltpu.VMEM((SAMPLES, 1, padded), f32),
            pltpu.VMEM((SAMPLES, 1, 3 * LANES), f32),
            pltpu.VMEM((SAMPLES, 1, 3 * LANES), f32),
            pltpu.VMEM((PEERS, 2, 1, 3 * LANES), f32),
            pltpu.VMEM((2, 1, 3 * LANES), f32),
            pltpu.VMEM((SAMPLES, 1, 3 * LANES), f32),
            pltpu.VMEM((SAMPLES, 1, padded), f32),
            pltpu.VMEM((SAMPLES, 1, padded), f32),
            pltpu.VMEM((1, hidden.shape[1]), f32),
            pltpu.VMEM(hidden.shape, f32),
            pltpu.VMEM((hidden.shape[0], LANES), f32),
            pltpu.SemaphoreType.DMA((7, PEERS)),
            pltpu.SemaphoreType.DMA((7, PEERS)),
            pltpu.SemaphoreType.DMA((7,)),
            pltpu.SemaphoreType.DMA((3, SAMPLES)),
            pltpu.SemaphoreType.DMA((3, SAMPLES)),
            pltpu.SemaphoreType.DMA((2, PEERS)),
            pltpu.SemaphoreType.DMA((2, PEERS)),
        ],
        compiler_params=pltpu.CompilerParams(
            collective_id=0, has_side_effects=True, vmem_limit_bytes=50 * 2**20
        ),
        cost_estimate=pl.CostEstimate(
            flops=10 * tokens * tokens * HEAD_DIM,
            bytes_accessed=14 * rows * width,
            transcendentals=tokens * tokens,
        ),
    )(cond, weight, hidden, incoming, q, k, v, g)


def per_device(cond_vec, mod_weight, text_hidden, text_grad, queries, keys, values, out_grad):
    grads = joint(
        cond_vec, mod_weight, text_hidden[0], text_grad[0],
        queries[0], keys[0], values[0], out_grad[0],
    )
    hidden_grad, weight_grad, cond_grad, query_grad, key_grad, value_grad = grads
    return (
        hidden_grad[None], weight_grad, cond_grad,
        query_grad[None], key_grad[None], value_grad[None],
    )


def solution(mesh):
    tokens = P("dp", "seq", None)
    weights = P(None, "seq", "dp")
    return jax.shard_map(
        per_device,
        mesh=mesh,
        in_specs=(P("dp", "seq"), weights, tokens, tokens, tokens, tokens, tokens, tokens),
        out_specs=(tokens, weights, P("dp", "seq"), tokens, tokens, tokens),
        check_vma=False,
    )
```

```python
import math

import jax
import jax.numpy as jnp
from jax import lax
from jax.experimental import pallas as pl
from jax.experimental.pallas import tpu as pltpu
from jax.sharding import PartitionSpec as P

HEADS = 16
HEAD_DIM = 128
NORM_EPS = 1e-06
PEERS = 16
SAMPLES = 32
LANES = 128
BLOCK = 4
CHUNK = 256
LOG2E = math.log2(math.e)
MESH = pl.DeviceIdType.MESH


def place_to(me, s):
    return ((me // 4 + s % 4) % 4) * 4 + (me % 4 + s // 4) % 4


def place_from(me, s):
    return ((me // 4 + 4 - s % 4) % 4) * 4 + (me % 4 + 4 - s // 4) % 4


def nt(a, b):
    return lax.dot_general(a, b, (((1,), (1,)), ((), ())), preferred_element_type=jnp.float32)


def nn(a, b):
    return lax.dot_general(a, b, (((1,), (0,)), ((), ())), preferred_element_type=jnp.float32)


def joint_kernel(
    cond_in, weight_in, hidden_in, incoming_in, q_ref, k_ref, v_ref, g_ref,
    hidden_grad_out, weight_grad_out, cond_grad_out, dq_ref, dk_ref, dv_ref,
    cond_ref, weight_ref, hidden_ref, incoming_ref, hidden_grad_ref, weight_grad_ref, cond_grad_ref,
    qb, kb, vb, gb, kt, u, dp, dka, dva, dqo, dko, dvo,
    cond_own, cond_all, parcel, parcels, partial, share, whole, back, backs, row, normed, spread,
    send, recv, local, dp_send, dp_recv, seq_send, seq_recv,
):
    rows = q_ref.shape[0]
    width = qb.shape[2]
    tokens = PEERS * rows
    chunks = tokens // CHUNK
    block = BLOCK * rows
    factor = width ** (-0.5)
    me = lax.axis_index("seq")
    mine = lax.axis_index("dp")
    weight_rows, columns = weight_ref.shape[1:]
    features = hidden_ref.shape[1]
    text_rows = hidden_ref.shape[0]

    def head_of(device):
        return pl.ds(pl.multiple_of(device * width, width), width)

    ins = ((k_ref, kb), (v_ref, vb), (q_ref, qb), (g_ref, gb))
    outs = ((dqo, dq_ref), (dko, dk_ref), (dvo, dv_ref))

    def inward(a, s):
        src, dst = ins[a]
        to = place_to(me, s)
        return pltpu.make_async_remote_copy(
            src.at[:, head_of(to)], dst.at[s], send.at[a, s], recv.at[a, s],
            device_id={"seq": to}, device_id_type=MESH,
        )

    def outward(a, s):
        src, dst = outs[a]
        return pltpu.make_async_remote_copy(
            src.at[s], dst.at[:, head_of(me)], send.at[4 + a, s], recv.at[4 + a, s],
            device_id={"seq": place_from(me, s)}, device_id_type=MESH,
        )

    def own_in(a):
        src, dst = ins[a]
        return pltpu.make_async_copy(src.at[:, head_of(me)], dst.at[0], local.at[a])

    def own_out(a):
        src, dst = outs[a]
        return pltpu.make_async_copy(src.at[0], dst.at[:, head_of(me)], local.at[4 + a])

    fetched = ((cond_in, cond_ref), (hidden_in, hidden_ref), (incoming_in, incoming_ref),
               (weight_in, weight_ref))
    kept = ((weight_grad_ref, weight_grad_out), (hidden_grad_ref, hidden_grad_out),
            (cond_grad_ref, cond_grad_out))

    def fetch(a):
        return pltpu.make_async_copy(*fetched[a], local.at[7 + a])

    def keep(a):
        return pltpu.make_async_copy(*kept[a], local.at[11 + a])

    def other(r):
        return (mine + r) % SAMPLES

    def dp_copy(step, r, arriving):
        src = (cond_own, parcel.at[other(r)], back.at[other(r)])[step]
        dst = (cond_all, parcels, backs)[step]
        place = other(r) if arriving else mine
        return pltpu.make_async_remote_copy(
            src, dst.at[place], dp_send.at[step, r], dp_recv.at[step, place],
            device_id={"dp": other(r)}, device_id_type=MESH,
        )

    def scatter_copy(s):
        to = place_to(me, s)
        return pltpu.make_async_remote_copy(
            parcels.at[pl.ds(to * 2, 2)], partial.at[s], seq_send.at[0, s], seq_recv.at[0, s],
            device_id={"seq": to}, device_id_type=MESH,
        )

    def gather_copy(s, arriving):
        place = place_from(me, s) if arriving else me
        return pltpu.make_async_remote_copy(
            share, whole.at[pl.ds(place * 2, 2)], seq_send.at[1, s], seq_recv.at[1, s],
            device_id={"seq": place_to(me, s)}, device_id_type=MESH,
        )

    def each(low, high, action):
        pl.loop(low, high)(action)

    for a in range(4):
        fetch(a).start()
    for a in range(4):
        own_in(a).start()

    barrier = pltpu.get_barrier_semaphore()

    @pl.loop(1, SAMPLES)
    def _(r):
        pl.semaphore_signal(barrier, inc=1, device_id={"dp": other(r)}, device_id_type=MESH)

    @pl.loop(1, PEERS)
    def _(s):
        pl.semaphore_signal(
            barrier, inc=1, device_id={"seq": place_to(me, s)}, device_id_type=MESH
        )

    cond_own[...] = jnp.zeros_like(cond_own)
    fetch(0).wait()
    cond_own[:, :weight_rows] = cond_ref[...]
    pl.semaphore_wait(barrier, PEERS + SAMPLES - 2)

    each(1, SAMPLES, lambda r: dp_copy(0, r, False).start())
    each(1, PEERS, lambda s: inward(0, s).start())

    fetch(1).wait()
    fetch(2).wait()
    plain = jnp.zeros((8, features), jnp.float32)
    scaled = jnp.zeros((8, features), jnp.float32)
    for t in range(0, text_rows, 16):
        at = slice(t, t + 16)
        hidden = hidden_ref[at].astype(jnp.float32)
        incoming = incoming_ref[at].astype(jnp.float32)
        centred = hidden - jnp.sum(hidden, axis=-1, keepdims=True) * (1.0 / features)
        variance = jnp.sum(centred * centred, axis=-1, keepdims=True) * (1.0 / features)
        inv_std = lax.rsqrt(variance + NORM_EPS)
        norm = centred * inv_std
        normed[at] = norm
        spread[at] = jnp.broadcast_to(inv_std, (16, LANES))
        plain += jnp.sum(incoming.reshape(2, 8, features), axis=0)
        scaled += jnp.sum((incoming * norm).reshape(2, 8, features), axis=0)
    plain = jnp.sum(plain, axis=0, keepdims=True)
    scaled = jnp.sum(scaled, axis=0, keepdims=True)
    parcel[...] = jnp.zeros_like(parcel)
    back[...] = jnp.zeros_like(back)
    for p in range(SAMPLES):
        at = slice(p * columns, (p + 1) * columns)
        parcel[p, :, LANES : LANES + columns] = plain[:, at]
        parcel[p, :, 2 * LANES : 2 * LANES + columns] = scaled[:, at]

    cond_all[mine] = cond_own[...]
    each(1, SAMPLES, lambda r: dp_copy(0, r, True).wait_recv())
    cond = cond_all[...].reshape(SAMPLES, cond_all.shape[2])[:, :weight_rows]
    act = (cond * jax.nn.sigmoid(cond)).astype(jnp.bfloat16)
    fetch(3).wait()
    parcel[:, :, :columns] = nn(act, weight_ref[1]).reshape(SAMPLES, 1, columns)
    each(1, SAMPLES, lambda r: dp_copy(1, r, False).start())
    each(1, PEERS, lambda s: inward(1, s).start())

    def send_block(i):
        for s in range(max(i * BLOCK, 1), (i + 1) * BLOCK):
            inward(2, s).start()
            inward(3, s).start()

    def scatter_sums():
        parcels[mine] = parcel[mine]
        each(1, SAMPLES, lambda r: dp_copy(1, r, True).wait_recv())
        each(1, PEERS, lambda s: scatter_copy(s).start())

    def gather_sums():
        partial[0] = parcels[pl.ds(me * 2, 2)]
        each(1, PEERS, lambda s: scatter_copy(s).wait_recv())
        share[...] = jnp.sum(partial[...], axis=0)
        each(1, PEERS, lambda s: gather_copy(s, False).start())

    def weight_gradients():
        whole[pl.ds(me * 2, 2)] = share[...]
        each(1, PEERS, lambda s: gather_copy(s, True).wait_recv())
        sums = whole[...].reshape(SAMPLES, whole.shape[2])
        cond = cond_all[...].reshape(SAMPLES, cond_all.shape[2])[:, :weight_rows]
        act = (cond * jax.nn.sigmoid(cond)).astype(jnp.bfloat16).astype(jnp.float32)
        backward = jnp.zeros((SAMPLES, weight_rows), jnp.float32)
        for k in range(2):
            grad = sums[:, (k + 1) * LANES : (k + 1) * LANES + columns]
            weight_grad_ref[k] = lax.dot_general(
                act, grad, (((0,), (0,)), ((), ())),
                precision=lax.Precision.HIGHEST, preferred_element_type=jnp.float32,
            )
            backward += lax.dot_general(
                grad, weight_ref[k].astype(jnp.float32), (((1,), (1,)), ((), ())),
                precision=lax.Precision.HIGHEST, preferred_element_type=jnp.float32,
            )
        keep(0).start()
        back[:, :, :weight_rows] = backward.reshape(SAMPLES, 1, weight_rows)
        each(1, SAMPLES, lambda r: dp_copy(2, r, False).start())

    def text_gradient():
        for j in range(SAMPLES):
            row[:, j * columns : (j + 1) * columns] = whole[j, :, :columns]
        gain = 1.0 + row[...]
        for t in range(0, text_rows, 16):
            at = slice(t, t + 16)
            norm = normed[at]
            upstream = incoming_ref[at].astype(jnp.float32) * gain
            mean = jnp.sum(upstream, axis=-1, keepdims=True) * (1.0 / features)
            along = jnp.sum(upstream * norm, axis=-1, keepdims=True) * (1.0 / features)
            grad = spread[at, :1] * (upstream - mean - norm * along)
            hidden_grad_ref[at] = grad.astype(jnp.bfloat16)
        keep(1).start()

    def cond_gradient():
        backs[mine] = back[mine]
        each(1, SAMPLES, lambda r: dp_copy(2, r, True).wait_recv())
        summed = jnp.sum(backs[...], axis=0)[:, :weight_rows]
        cond = cond_ref[...]
        sigma = jax.nn.sigmoid(cond)
        cond_grad_ref[...] = summed * sigma * (1.0 + cond * (1.0 - sigma))
        keep(2).start()

    dka[...] = jnp.zeros_like(dka)
    dva[...] = jnp.zeros_like(dva)
    for a in range(4):
        own_in(a).wait()
    each(1, PEERS, lambda s: inward(0, s).wait_recv())

    for s in range(PEERS):
        kt[:, s * rows : (s + 1) * rows] = kb[s].astype(jnp.float32).T.astype(jnp.bfloat16)

    scatter_sums()
    send_block(0)
    each(1, PEERS, lambda s: inward(1, s).wait_recv())
    gather_sums()
    send_block(1)
    send_block(2)

    per_chunk = CHUNK // rows

    @pl.loop(0, PEERS // BLOCK)
    def _(i):
        first = i * BLOCK
        for j in range(BLOCK):

            @pl.when(first + j > 0)
            def _():
                inward(2, first + j).wait_recv()
                inward(3, first + j).wait_recv()

        here = pl.ds(pl.multiple_of(first, BLOCK), BLOCK)
        queries = qb[here].reshape(block, width)
        grads = gb[here].reshape(block, width)
        peak = None
        for t in range(chunks):
            keys = kb[t * per_chunk : (t + 1) * per_chunk].reshape(CHUNK, width)
            scores = nt(keys, queries)
            u[t] = scores
            top = jnp.max(scores.reshape(CHUNK // 8, 8, block), axis=0)
            peak = top if peak is None else jnp.maximum(peak, top)
        peak = jnp.max(peak, axis=0, keepdims=True)
        total = jnp.zeros((8, block), jnp.float32)
        delta = jnp.zeros((8, block), jnp.float32)
        for t in range(chunks):
            values = vb[t * per_chunk : (t + 1) * per_chunk].reshape(CHUNK, width)
            prob_grad = nt(values, grads)
            exponent = jnp.exp2((u[t] - peak) * (factor * LOG2E))
            total += jnp.sum(exponent.reshape(CHUNK // 8, 8, block), axis=0)
            delta += jnp.sum((exponent * prob_grad).reshape(CHUNK // 8, 8, block), axis=0)
            u[t] = exponent
            dp[t] = prob_grad
        inverse = 1.0 / jnp.sum(total, axis=0, keepdims=True)
        delta = jnp.sum(delta, axis=0, keepdims=True) * inverse
        query_grad = jnp.zeros((width, block), jnp.float32)
        for t in range(chunks):
            at = slice(t * CHUNK, (t + 1) * CHUNK)
            probability = u[t] * inverse
            score_low = (probability * (dp[t] - delta)).astype(jnp.bfloat16)
            dva[at] += nn(probability.astype(jnp.bfloat16), grads)
            dka[at] += nn(score_low, queries)
            query_grad += nn(kt[:, at], score_low)
        dqo[here] = (
            (query_grad * factor).T.astype(jnp.bfloat16).reshape(BLOCK, rows, width)
        )
        for j in range(BLOCK):

            @pl.when(first + j > 0)
            def _():
                outward(0, first + j).start()

        @pl.when(i == 0)
        def _():
            weight_gradients()
            send_block(3)

    own_out(0).start()
    for s in range(PEERS):
        at = slice(s * rows, (s + 1) * rows)
        dko[s] = (dka[at] * factor).astype(jnp.bfloat16)
        dvo[s] = dva[at].astype(jnp.bfloat16)

    @pl.loop(1, PEERS)
    def _(s):
        outward(1, s).start()
        outward(2, s).start()

    own_out(1).start()
    own_out(2).start()
    text_gradient()
    cond_gradient()

    @pl.loop(1, SAMPLES)
    def _(r):
        for step in range(3):
            dp_copy(step, r, False).wait_send()

    @pl.loop(1, PEERS)
    def _(s):
        scatter_copy(s).wait_send()
        gather_copy(s, False).wait_send()

    @pl.loop(1, PEERS)
    def _(s):
        for a in range(4):
            inward(a, s).wait_send()
        for a in range(3):
            outward(a, s).wait_send()

    for a in range(3):
        own_out(a).wait()
        keep(a).wait()

    @pl.loop(1, PEERS)
    def _(s):
        for a in range(3):
            outward(a, s).wait_recv()


def joint(cond, weight, hidden, incoming, q, k, v, g):
    rows, width = q.shape
    slots = pltpu.VMEM((PEERS, rows, HEAD_DIM), jnp.bfloat16)
    tokens = PEERS * rows
    scores = pltpu.VMEM((tokens // CHUNK, CHUNK, BLOCK * rows), jnp.float32)
    total = pltpu.VMEM((tokens, HEAD_DIM), jnp.float32)
    anywhere = pl.BlockSpec(memory_space=pl.ANY)
    padded = -(-cond.shape[1] // LANES) * LANES
    f32 = jnp.float32
    return pl.pallas_call(
        joint_kernel,
        out_shape=[
            jax.ShapeDtypeStruct(hidden.shape, jnp.bfloat16),
            jax.ShapeDtypeStruct(weight.shape, f32),
            jax.ShapeDtypeStruct(cond.shape, f32),
        ]
        + [jax.ShapeDtypeStruct((rows, width), jnp.bfloat16)] * 3,
        in_specs=[anywhere] * 8,
        out_specs=[anywhere] * 6,
        scratch_shapes=[
            pltpu.VMEM(cond.shape, f32),
            pltpu.VMEM(weight.shape, jnp.bfloat16),
            pltpu.VMEM(hidden.shape, jnp.bfloat16),
            pltpu.VMEM(hidden.shape, jnp.bfloat16),
            pltpu.VMEM(hidden.shape, jnp.bfloat16),
            pltpu.VMEM(weight.shape, f32),
            pltpu.VMEM(cond.shape, f32),
            slots, slots, slots, slots,
            pltpu.VMEM((HEAD_DIM, tokens), jnp.bfloat16),
            scores, scores, total, total,
            slots, slots, slots,
            pltpu.VMEM((1, padded), f32),
            pltpu.VMEM((SAMPLES, 1, padded), f32),
            pltpu.VMEM((SAMPLES, 1, 3 * LANES), f32),
            pltpu.VMEM((SAMPLES, 1, 3 * LANES), f32),
            pltpu.VMEM((PEERS, 2, 1, 3 * LANES), f32),
            pltpu.VMEM((2, 1, 3 * LANES), f32),
            pltpu.VMEM((SAMPLES, 1, 3 * LANES), f32),
            pltpu.VMEM((SAMPLES, 1, padded), f32),
            pltpu.VMEM((SAMPLES, 1, padded), f32),
            pltpu.VMEM((1, hidden.shape[1]), f32),
            pltpu.VMEM(hidden.shape, f32),
            pltpu.VMEM((hidden.shape[0], LANES), f32),
            pltpu.SemaphoreType.DMA((7, PEERS)),
            pltpu.SemaphoreType.DMA((7, PEERS)),
            pltpu.SemaphoreType.DMA((14,)),
            pltpu.SemaphoreType.DMA((3, SAMPLES)),
            pltpu.SemaphoreType.DMA((3, SAMPLES)),
            pltpu.SemaphoreType.DMA((2, PEERS)),
            pltpu.SemaphoreType.DMA((2, PEERS)),
        ],
        compiler_params=pltpu.CompilerParams(
            collective_id=0, has_side_effects=True, vmem_limit_bytes=62 * 2**20
        ),
        cost_estimate=pl.CostEstimate(
            flops=10 * tokens * tokens * HEAD_DIM,
            bytes_accessed=14 * rows * width,
            transcendentals=tokens * tokens,
        ),
    )(cond, weight, hidden, incoming, q, k, v, g)


def deliver_kernel(*refs):
    count = (len(refs) - 2) // 3
    sources, results, passing = refs[:count], refs[count : 2 * count], refs[2 * count : 3 * count]
    arrived, done = refs[3 * count :]
    loads = [pltpu.make_async_copy(sources[n], passing[n], arrived.at[n]) for n in range(count)]
    stores = [pltpu.make_async_copy(passing[n], results[n], done.at[n]) for n in range(count)]
    for load in loads:
        load.start()
    for load, store in zip(loads, stores):
        load.wait()
        store.start()
    for store in stores:
        store.wait()


def deliver(results):
    anywhere = pl.BlockSpec(memory_space=pl.ANY)
    return pl.pallas_call(
        deliver_kernel,
        out_shape=[jax.ShapeDtypeStruct(r.shape, r.dtype) for r in results],
        in_specs=[anywhere] * len(results),
        out_specs=[anywhere] * len(results),
        scratch_shapes=[pltpu.VMEM(r.shape, r.dtype) for r in results]
        + [pltpu.SemaphoreType.DMA((len(results),))] * 2,
        compiler_params=pltpu.CompilerParams(vmem_limit_bytes=62 * 2**20),
    )(*results)


def per_device(cond_vec, mod_weight, text_hidden, text_grad, queries, keys, values, out_grad):
    grads = joint(
        cond_vec, mod_weight, text_hidden[0], text_grad[0],
        queries[0], keys[0], values[0], out_grad[0],
    )
    grads = deliver(grads)
    hidden_grad, weight_grad, cond_grad, query_grad, key_grad, value_grad = grads
    return (
        hidden_grad[None], weight_grad, cond_grad,
        query_grad[None], key_grad[None], value_grad[None],
    )


def solution(mesh):
    tokens = P("dp", "seq", None)
    weights = P(None, "seq", "dp")
    return jax.shard_map(
        per_device,
        mesh=mesh,
        in_specs=(P("dp", "seq"), weights, tokens, tokens, tokens, tokens, tokens, tokens),
        out_specs=(tokens, weights, P("dp", "seq"), tokens, tokens, tokens),
        check_vma=False,
    )
```

```python
import math

import jax
import jax.numpy as jnp
from jax import lax
from jax.experimental import pallas as pl
from jax.experimental.pallas import tpu as pltpu
from jax.sharding import PartitionSpec as P

HEADS = 16
HEAD_DIM = 128
NORM_EPS = 1e-06
PEERS = 16
SAMPLES = 32
LANES = 128
HIGH, LOW = 4, 8
BLOCK = 4
CHUNK = 256
LOG2E = math.log2(math.e)
MESH = pl.DeviceIdType.MESH


def place_to(me, s):
    return ((me // 4 + s % 4) % 4) * 4 + (me % 4 + s // 4) % 4


def place_from(me, s):
    return ((me // 4 + 4 - s % 4) % 4) * 4 + (me % 4 + 4 - s // 4) % 4


def rank_of(device):
    return device % LOW * HIGH + device // LOW


def device_of(rank):
    return rank % HIGH * LOW + rank // HIGH


def nt(a, b):
    return lax.dot_general(a, b, (((1,), (1,)), ((), ())), preferred_element_type=jnp.float32)


def nn(a, b):
    return lax.dot_general(a, b, (((1,), (0,)), ((), ())), preferred_element_type=jnp.float32)


def joint_kernel(
    cond_in, weight_in, hidden_in, incoming_in, q_ref, k_ref, v_ref, g_ref,
    hidden_grad_out, weight_grad_out, cond_grad_out, dq_ref, dk_ref, dv_ref,
    cond_ref, weight_ref, hidden_ref, incoming_ref, hidden_grad_ref, weight_grad_ref, cond_grad_ref,
    qb, kb, vb, gb, kt, u, dp, dka, dva, dqo, dko, dvo,
    cond_own, cond_all, parcel, parcels, partial, share, whole, back, halves, half, backs,
    row, normed, spread,
    send, recv, local, dp_send, dp_recv, low_send, low_recv, high_send, high_recv,
    seq_send, seq_recv,
):
    rows = q_ref.shape[0]
    width = qb.shape[2]
    tokens = PEERS * rows
    chunks = tokens // CHUNK
    block = BLOCK * rows
    factor = width ** (-0.5)
    me = lax.axis_index("seq")
    mine = lax.axis_index("dp")
    low, high = mine % LOW, mine // LOW
    weight_rows, columns = weight_ref.shape[1:]
    features = hidden_ref.shape[1]
    text_rows = hidden_ref.shape[0]

    def head_of(device):
        return pl.ds(pl.multiple_of(device * width, width), width)

    ins = ((k_ref, kb), (v_ref, vb), (q_ref, qb), (g_ref, gb))
    outs = ((dqo, dq_ref), (dko, dk_ref), (dvo, dv_ref))

    def inward(a, s):
        src, dst = ins[a]
        to = place_to(me, s)
        return pltpu.make_async_remote_copy(
            src.at[:, head_of(to)], dst.at[s], send.at[a, s], recv.at[a, s],
            device_id={"seq": to}, device_id_type=MESH,
        )

    def outward(a, s):
        src, dst = outs[a]
        return pltpu.make_async_remote_copy(
            src.at[s], dst.at[:, head_of(me)], send.at[4 + a, s], recv.at[4 + a, s],
            device_id={"seq": place_from(me, s)}, device_id_type=MESH,
        )

    def own_in(a):
        src, dst = ins[a]
        return pltpu.make_async_copy(src.at[:, head_of(me)], dst.at[0], local.at[a])

    def own_out(a):
        src, dst = outs[a]
        return pltpu.make_async_copy(src.at[0], dst.at[:, head_of(me)], local.at[4 + a])

    fetched = ((cond_in, cond_ref), (hidden_in, hidden_ref), (incoming_in, incoming_ref),
               (weight_in, weight_ref))
    kept = ((weight_grad_ref, weight_grad_out), (hidden_grad_ref, hidden_grad_out),
            (cond_grad_ref, cond_grad_out))

    def fetch(a):
        return pltpu.make_async_copy(*fetched[a], local.at[7 + a])

    def keep(a):
        return pltpu.make_async_copy(*kept[a], local.at[11 + a])

    def other(r):
        return (mine + r) % SAMPLES

    def dp_copy(r, arriving):
        there = rank_of(other(r))
        place = there if arriving else rank_of(mine)
        return pltpu.make_async_remote_copy(
            parcel.at[there], parcels.at[place], dp_send.at[r], dp_recv.at[place],
            device_id={"dp": other(r)}, device_id_type=MESH,
        )

    def high_copy(step, h, arriving):
        there = (high + h) % HIGH
        place = there if arriving else high
        src = (cond_own, half.at[there])[step]
        dst = (cond_all.at[low, place], backs.at[place])[step]
        return pltpu.make_async_remote_copy(
            src, dst, high_send.at[step, h], high_recv.at[step, place],
            device_id={"dp": there * LOW + low}, device_id_type=MESH,
        )

    def low_copy(step, r, arriving):
        there = (low + r) % LOW
        place = there if arriving else low
        src = (cond_all.at[low], back.at[there])[step]
        dst = (cond_all.at[place], halves.at[place])[step]
        return pltpu.make_async_remote_copy(
            src, dst, low_send.at[step, r], low_recv.at[step, place],
            device_id={"dp": high * LOW + there}, device_id_type=MESH,
        )

    def scatter_copy(s):
        to = place_to(me, s)
        return pltpu.make_async_remote_copy(
            parcels.at[pl.ds(to * 2, 2)], partial.at[s], seq_send.at[0, s], seq_recv.at[0, s],
            device_id={"seq": to}, device_id_type=MESH,
        )

    def gather_copy(s, arriving):
        place = place_from(me, s) if arriving else me
        return pltpu.make_async_remote_copy(
            share, whole.at[pl.ds(place * 2, 2)], seq_send.at[1, s], seq_recv.at[1, s],
            device_id={"seq": place_to(me, s)}, device_id_type=MESH,
        )

    def each(low, high, action):
        pl.loop(low, high)(action)

    for a in range(4):
        fetch(a).start()
    for a in range(4):
        own_in(a).start()

    barrier = pltpu.get_barrier_semaphore()

    @pl.loop(1, SAMPLES)
    def _(r):
        pl.semaphore_signal(barrier, inc=1, device_id={"dp": other(r)}, device_id_type=MESH)

    @pl.loop(1, PEERS)
    def _(s):
        pl.semaphore_signal(
            barrier, inc=1, device_id={"seq": place_to(me, s)}, device_id_type=MESH
        )

    cond_own[...] = jnp.zeros_like(cond_own)
    fetch(0).wait()
    cond_own[:, :weight_rows] = cond_ref[...]
    pl.semaphore_wait(barrier, PEERS + SAMPLES - 2)

    each(1, HIGH, lambda h: high_copy(0, h, False).start())
    each(1, PEERS, lambda s: inward(0, s).start())
    cond_all[low, high] = cond_own[...]

    each(1, HIGH, lambda h: high_copy(0, h, True).wait_recv())
    each(1, LOW, lambda r: low_copy(0, r, False).start())

    fetch(1).wait()
    fetch(2).wait()
    plain = jnp.zeros((8, features), jnp.float32)
    scaled = jnp.zeros((8, features), jnp.float32)
    for t in range(0, text_rows, 16):
        at = slice(t, t + 16)
        hidden = hidden_ref[at].astype(jnp.float32)
        incoming = incoming_ref[at].astype(jnp.float32)
        centred = hidden - jnp.sum(hidden, axis=-1, keepdims=True) * (1.0 / features)
        variance = jnp.sum(centred * centred, axis=-1, keepdims=True) * (1.0 / features)
        inv_std = lax.rsqrt(variance + NORM_EPS)
        norm = centred * inv_std
        normed[at] = norm
        spread[at] = jnp.broadcast_to(inv_std, (16, LANES))
        plain += jnp.sum(incoming.reshape(2, 8, features), axis=0)
        scaled += jnp.sum((incoming * norm).reshape(2, 8, features), axis=0)
    plain = jnp.sum(plain, axis=0, keepdims=True)
    scaled = jnp.sum(scaled, axis=0, keepdims=True)
    parcel[...] = jnp.zeros_like(parcel)
    back[...] = jnp.zeros_like(back)
    for p in range(SAMPLES):
        first = device_of(p) * columns
        at = slice(first, first + columns)
        parcel[p, :, LANES : LANES + columns] = plain[:, at]
        parcel[p, :, 2 * LANES : 2 * LANES + columns] = scaled[:, at]

    each(1, LOW, lambda r: low_copy(0, r, True).wait_recv())
    cond = cond_all[...].reshape(SAMPLES, cond_all.shape[3])[:, :weight_rows]
    act = (cond * jax.nn.sigmoid(cond)).astype(jnp.bfloat16)
    fetch(3).wait()
    parcel[:, :, :columns] = nn(act, weight_ref[1]).reshape(SAMPLES, 1, columns)
    each(1, SAMPLES, lambda r: dp_copy(r, False).start())
    each(1, PEERS, lambda s: inward(1, s).start())

    def send_block(i):
        for s in range(max(i * BLOCK, 1), (i + 1) * BLOCK):
            inward(2, s).start()
            inward(3, s).start()

    def scatter_sums():
        parcels[rank_of(mine)] = parcel[rank_of(mine)]
        each(1, SAMPLES, lambda r: dp_copy(r, True).wait_recv())
        each(1, PEERS, lambda s: scatter_copy(s).start())

    def gather_sums():
        partial[0] = parcels[pl.ds(me * 2, 2)]
        each(1, PEERS, lambda s: scatter_copy(s).wait_recv())
        share[...] = jnp.sum(partial[...], axis=0)
        each(1, PEERS, lambda s: gather_copy(s, False).start())

    def weight_gradients():
        whole[pl.ds(me * 2, 2)] = share[...]
        each(1, PEERS, lambda s: gather_copy(s, True).wait_recv())
        sums = whole[...].reshape(SAMPLES, whole.shape[2])
        cond = cond_all[...].reshape(SAMPLES, cond_all.shape[3])[:, :weight_rows]
        act = (cond * jax.nn.sigmoid(cond)).astype(jnp.bfloat16).astype(jnp.float32)
        backward = jnp.zeros((SAMPLES, weight_rows), jnp.float32)
        for k in range(2):
            grad = sums[:, (k + 1) * LANES : (k + 1) * LANES + columns]
            weight_grad_ref[k] = lax.dot_general(
                act, grad, (((0,), (0,)), ((), ())),
                precision=lax.Precision.HIGHEST, preferred_element_type=jnp.float32,
            )
            backward += lax.dot_general(
                grad, weight_ref[k].astype(jnp.float32), (((1,), (1,)), ((), ())),
                precision=lax.Precision.HIGHEST, preferred_element_type=jnp.float32,
            )
        keep(0).start()
        back[:, :, :, :weight_rows] = backward.reshape(LOW, HIGH, 1, weight_rows)
        each(1, LOW, lambda r: low_copy(1, r, False).start())

    def half_sums():
        halves[low] = back[low]
        each(1, LOW, lambda r: low_copy(1, r, True).wait_recv())
        half[...] = jnp.sum(halves[...], axis=0)
        each(1, HIGH, lambda h: high_copy(1, h, False).start())

    def text_gradient():
        for j in range(SAMPLES):
            first = device_of(j) * columns
            row[:, first : first + columns] = whole[j, :, :columns]
        gain = 1.0 + row[...]
        for t in range(0, text_rows, 16):
            at = slice(t, t + 16)
            norm = normed[at]
            upstream = incoming_ref[at].astype(jnp.float32) * gain
            mean = jnp.sum(upstream, axis=-1, keepdims=True) * (1.0 / features)
            along = jnp.sum(upstream * norm, axis=-1, keepdims=True) * (1.0 / features)
            grad = spread[at, :1] * (upstream - mean - norm * along)
            hidden_grad_ref[at] = grad.astype(jnp.bfloat16)
        keep(1).start()

    def cond_gradient():
        backs[high] = half[high]
        each(1, HIGH, lambda h: high_copy(1, h, True).wait_recv())
        summed = jnp.sum(backs[...], axis=0)[:, :weight_rows]
        cond = cond_ref[...]
        sigma = jax.nn.sigmoid(cond)
        cond_grad_ref[...] = summed * sigma * (1.0 + cond * (1.0 - sigma))
        keep(2).start()

    dka[...] = jnp.zeros_like(dka)
    dva[...] = jnp.zeros_like(dva)
    for a in range(4):
        own_in(a).wait()
    each(1, PEERS, lambda s: inward(0, s).wait_recv())

    for s in range(PEERS):
        kt[:, s * rows : (s + 1) * rows] = kb[s].astype(jnp.float32).T.astype(jnp.bfloat16)

    scatter_sums()
    send_block(0)
    each(1, PEERS, lambda s: inward(1, s).wait_recv())
    gather_sums()
    send_block(1)
    send_block(2)

    per_chunk = CHUNK // rows

    @pl.loop(0, PEERS // BLOCK)
    def _(i):
        first = i * BLOCK
        for j in range(BLOCK):

            @pl.when(first + j > 0)
            def _():
                inward(2, first + j).wait_recv()
                inward(3, first + j).wait_recv()

        here = pl.ds(pl.multiple_of(first, BLOCK), BLOCK)
        queries = qb[here].reshape(block, width)
        grads = gb[here].reshape(block, width)
        peak = None
        for t in range(chunks):
            keys = kb[t * per_chunk : (t + 1) * per_chunk].reshape(CHUNK, width)
            scores = nt(keys, queries)
            u[t] = scores
            top = jnp.max(scores.reshape(CHUNK // 8, 8, block), axis=0)
            peak = top if peak is None else jnp.maximum(peak, top)
        peak = jnp.max(peak, axis=0, keepdims=True)
        total = jnp.zeros((8, block), jnp.float32)
        delta = jnp.zeros((8, block), jnp.float32)
        for t in range(chunks):
            values = vb[t * per_chunk : (t + 1) * per_chunk].reshape(CHUNK, width)
            prob_grad = nt(values, grads)
            exponent = jnp.exp2((u[t] - peak) * (factor * LOG2E))
            total += jnp.sum(exponent.reshape(CHUNK // 8, 8, block), axis=0)
            delta += jnp.sum((exponent * prob_grad).reshape(CHUNK // 8, 8, block), axis=0)
            u[t] = exponent
            dp[t] = prob_grad
        inverse = 1.0 / jnp.sum(total, axis=0, keepdims=True)
        delta = jnp.sum(delta, axis=0, keepdims=True) * inverse
        query_grad = jnp.zeros((width, block), jnp.float32)
        for t in range(chunks):
            at = slice(t * CHUNK, (t + 1) * CHUNK)
            probability = u[t] * inverse
            score_low = (probability * (dp[t] - delta)).astype(jnp.bfloat16)
            dva[at] += nn(probability.astype(jnp.bfloat16), grads)
            dka[at] += nn(score_low, queries)
            query_grad += nn(kt[:, at], score_low)
        dqo[here] = (
            (query_grad * factor).T.astype(jnp.bfloat16).reshape(BLOCK, rows, width)
        )
        for j in range(BLOCK):

            @pl.when(first + j > 0)
            def _():
                outward(0, first + j).start()

        @pl.when(i == 0)
        def _():
            weight_gradients()
            send_block(3)

        pl.when(i == 1)(half_sums)

    own_out(0).start()
    for s in range(PEERS):
        at = slice(s * rows, (s + 1) * rows)
        dko[s] = (dka[at] * factor).astype(jnp.bfloat16)
        dvo[s] = dva[at].astype(jnp.bfloat16)

    @pl.loop(1, PEERS)
    def _(s):
        outward(1, s).start()
        outward(2, s).start()

    own_out(1).start()
    own_out(2).start()
    text_gradient()
    cond_gradient()

    @pl.loop(1, SAMPLES)
    def _(r):
        dp_copy(r, False).wait_send()

    for step in range(2):
        each(1, HIGH, lambda h: high_copy(step, h, False).wait_send())
        each(1, LOW, lambda r: low_copy(step, r, False).wait_send())

    @pl.loop(1, PEERS)
    def _(s):
        scatter_copy(s).wait_send()
        gather_copy(s, False).wait_send()

    @pl.loop(1, PEERS)
    def _(s):
        for a in range(4):
            inward(a, s).wait_send()
        for a in range(3):
            outward(a, s).wait_send()

    for a in range(3):
        own_out(a).wait()
        keep(a).wait()

    @pl.loop(1, PEERS)
    def _(s):
        for a in range(3):
            outward(a, s).wait_recv()


def joint(cond, weight, hidden, incoming, q, k, v, g):
    rows, width = q.shape
    slots = pltpu.VMEM((PEERS, rows, HEAD_DIM), jnp.bfloat16)
    tokens = PEERS * rows
    scores = pltpu.VMEM((tokens // CHUNK, CHUNK, BLOCK * rows), jnp.float32)
    total = pltpu.VMEM((tokens, HEAD_DIM), jnp.float32)
    anywhere = pl.BlockSpec(memory_space=pl.ANY)
    padded = -(-cond.shape[1] // LANES) * LANES
    f32 = jnp.float32
    return pl.pallas_call(
        joint_kernel,
        out_shape=[
            jax.ShapeDtypeStruct(hidden.shape, jnp.bfloat16),
            jax.ShapeDtypeStruct(weight.shape, f32),
            jax.ShapeDtypeStruct(cond.shape, f32),
        ]
        + [jax.ShapeDtypeStruct((rows, width), jnp.bfloat16)] * 3,
        in_specs=[anywhere] * 8,
        out_specs=[anywhere] * 6,
        scratch_shapes=[
            pltpu.VMEM(cond.shape, f32),
            pltpu.VMEM(weight.shape, jnp.bfloat16),
            pltpu.VMEM(hidden.shape, jnp.bfloat16),
            pltpu.VMEM(hidden.shape, jnp.bfloat16),
            pltpu.VMEM(hidden.shape, jnp.bfloat16),
            pltpu.VMEM(weight.shape, f32),
            pltpu.VMEM(cond.shape, f32),
            slots, slots, slots, slots,
            pltpu.VMEM((HEAD_DIM, tokens), jnp.bfloat16),
            scores, scores, total, total,
            slots, slots, slots,
            pltpu.VMEM((1, padded), f32),
            pltpu.VMEM((LOW, HIGH, 1, padded), f32),
            pltpu.VMEM((SAMPLES, 1, 3 * LANES), f32),
            pltpu.VMEM((SAMPLES, 1, 3 * LANES), f32),
            pltpu.VMEM((PEERS, 2, 1, 3 * LANES), f32),
            pltpu.VMEM((2, 1, 3 * LANES), f32),
            pltpu.VMEM((SAMPLES, 1, 3 * LANES), f32),
            pltpu.VMEM((LOW, HIGH, 1, padded), f32),
            pltpu.VMEM((LOW, HIGH, 1, padded), f32),
            pltpu.VMEM((HIGH, 1, padded), f32),
            pltpu.VMEM((HIGH, 1, padded), f32),
            pltpu.VMEM((1, hidden.shape[1]), f32),
            pltpu.VMEM(hidden.shape, f32),
            pltpu.VMEM((hidden.shape[0], LANES), f32),
            pltpu.SemaphoreType.DMA((7, PEERS)),
            pltpu.SemaphoreType.DMA((7, PEERS)),
            pltpu.SemaphoreType.DMA((14,)),
            pltpu.SemaphoreType.DMA((SAMPLES,)),
            pltpu.SemaphoreType.DMA((SAMPLES,)),
            pltpu.SemaphoreType.DMA((2, LOW)),
            pltpu.SemaphoreType.DMA((2, LOW)),
            pltpu.SemaphoreType.DMA((2, HIGH)),
            pltpu.SemaphoreType.DMA((2, HIGH)),
            pltpu.SemaphoreType.DMA((2, PEERS)),
            pltpu.SemaphoreType.DMA((2, PEERS)),
        ],
        compiler_params=pltpu.CompilerParams(
            collective_id=0, has_side_effects=True, vmem_limit_bytes=62 * 2**20
        ),
        cost_estimate=pl.CostEstimate(
            flops=10 * tokens * tokens * HEAD_DIM,
            bytes_accessed=14 * rows * width,
            transcendentals=tokens * tokens,
        ),
    )(cond, weight, hidden, incoming, q, k, v, g)


def deliver_kernel(*refs):
    count = (len(refs) - 2) // 3
    sources, results, passing = refs[:count], refs[count : 2 * count], refs[2 * count : 3 * count]
    arrived, done = refs[3 * count :]
    loads = [pltpu.make_async_copy(sources[n], passing[n], arrived.at[n]) for n in range(count)]
    stores = [pltpu.make_async_copy(passing[n], results[n], done.at[n]) for n in range(count)]
    for load in loads:
        load.start()
    for load, store in zip(loads, stores):
        load.wait()
        store.start()
    for store in stores:
        store.wait()


def deliver(results):
    anywhere = pl.BlockSpec(memory_space=pl.ANY)
    return pl.pallas_call(
        deliver_kernel,
        out_shape=[jax.ShapeDtypeStruct(r.shape, r.dtype) for r in results],
        in_specs=[anywhere] * len(results),
        out_specs=[anywhere] * len(results),
        scratch_shapes=[pltpu.VMEM(r.shape, r.dtype) for r in results]
        + [pltpu.SemaphoreType.DMA((len(results),))] * 2,
        compiler_params=pltpu.CompilerParams(vmem_limit_bytes=62 * 2**20),
    )(*results)


def per_device(cond_vec, mod_weight, text_hidden, text_grad, queries, keys, values, out_grad):
    grads = joint(
        cond_vec, mod_weight, text_hidden[0], text_grad[0],
        queries[0], keys[0], values[0], out_grad[0],
    )
    grads = deliver(grads)
    hidden_grad, weight_grad, cond_grad, query_grad, key_grad, value_grad = grads
    return (
        hidden_grad[None], weight_grad, cond_grad,
        query_grad[None], key_grad[None], value_grad[None],
    )


def solution(mesh):
    tokens = P("dp", "seq", None)
    weights = P(None, "seq", "dp")
    return jax.shard_map(
        per_device,
        mesh=mesh,
        in_specs=(P("dp", "seq"), weights, tokens, tokens, tokens, tokens, tokens, tokens),
        out_specs=(tokens, weights, P("dp", "seq"), tokens, tokens, tokens),
        check_vma=False,
    )
```

```python
import math

import jax
import jax.numpy as jnp
from jax import lax
from jax.experimental import pallas as pl
from jax.experimental.pallas import tpu as pltpu
from jax.sharding import PartitionSpec as P

HEADS = 16
HEAD_DIM = 128
NORM_EPS = 1e-06
PEERS = 16
SAMPLES = 32
LANES = 128
HIGH, LOW = 4, 8
BLOCK = 4
CHUNK = 256
LOG2E = math.log2(math.e)
MESH = pl.DeviceIdType.MESH


def place_to(me, s):
    return ((me // 4 + s % 4) % 4) * 4 + (me % 4 + s // 4) % 4


def place_from(me, s):
    return ((me // 4 + 4 - s % 4) % 4) * 4 + (me % 4 + 4 - s // 4) % 4


def rank_of(device):
    return device % LOW * HIGH + device // LOW


def device_of(rank):
    return rank % HIGH * LOW + rank // HIGH


def nt(a, b):
    return lax.dot_general(a, b, (((1,), (1,)), ((), ())), preferred_element_type=jnp.float32)


def nn(a, b):
    return lax.dot_general(a, b, (((1,), (0,)), ((), ())), preferred_element_type=jnp.float32)


def joint_kernel(
    cond_in, weight_in, hidden_in, incoming_in, q_ref, k_ref, v_ref, g_ref,
    hidden_grad_out, weight_grad_out, cond_grad_out, dq_ref, dk_ref, dv_ref,
    cond_ref, weight_ref, hidden_ref, incoming_ref, hidden_grad_ref, weight_grad_ref, cond_grad_ref,
    qb, kb, vb, gb, kt, u, dp, dka, dva, dqo, dko, dvo,
    cond_own, cond_all, parcel, parcels, partial, share, whole, back, halves, half, backs,
    row, normed, spread,
    send, recv, local, dp_send, dp_recv, low_send, low_recv, high_send, high_recv,
    seq_send, seq_recv, entered, opened,
):
    rows = q_ref.shape[0]
    width = qb.shape[2]
    tokens = PEERS * rows
    chunks = tokens // CHUNK
    block = BLOCK * rows
    factor = width ** (-0.5)
    me = lax.axis_index("seq")
    mine = lax.axis_index("dp")
    low, high = mine % LOW, mine // LOW
    weight_rows, columns = weight_ref.shape[1:]
    features = hidden_ref.shape[1]
    text_rows = hidden_ref.shape[0]

    def head_of(device):
        return pl.ds(pl.multiple_of(device * width, width), width)

    ins = ((k_ref, kb), (v_ref, vb), (q_ref, qb), (g_ref, gb))
    outs = ((dqo, dq_ref), (dko, dk_ref), (dvo, dv_ref))

    def inward(a, s):
        src, dst = ins[a]
        to = place_to(me, s)
        return pltpu.make_async_remote_copy(
            src.at[:, head_of(to)], dst.at[s], send.at[a, s], recv.at[a, s],
            device_id={"seq": to}, device_id_type=MESH,
        )

    def outward(a, s):
        src, dst = outs[a]
        return pltpu.make_async_remote_copy(
            src.at[s], dst.at[:, head_of(me)], send.at[4 + a, s], recv.at[4 + a, s],
            device_id={"seq": place_from(me, s)}, device_id_type=MESH,
        )

    def own_in(a):
        src, dst = ins[a]
        return pltpu.make_async_copy(src.at[:, head_of(me)], dst.at[0], local.at[a])

    def own_out(a):
        src, dst = outs[a]
        return pltpu.make_async_copy(src.at[0], dst.at[:, head_of(me)], local.at[4 + a])

    fetched = ((cond_in, cond_ref), (hidden_in, hidden_ref), (incoming_in, incoming_ref),
               (weight_in, weight_ref))
    kept = ((weight_grad_ref, weight_grad_out), (hidden_grad_ref, hidden_grad_out),
            (cond_grad_ref, cond_grad_out))

    def fetch(a):
        return pltpu.make_async_copy(*fetched[a], local.at[7 + a])

    def keep(a):
        return pltpu.make_async_copy(*kept[a], local.at[11 + a])

    def other(r):
        return (mine + r) % SAMPLES

    def dp_copy(r, arriving):
        there = rank_of(other(r))
        place = there if arriving else rank_of(mine)
        return pltpu.make_async_remote_copy(
            parcel.at[there], parcels.at[place], dp_send.at[r], dp_recv.at[place],
            device_id={"dp": other(r)}, device_id_type=MESH,
        )

    def high_copy(step, h, arriving):
        there = (high + h) % HIGH
        place = there if arriving else high
        src = (cond_own, half.at[there])[step]
        dst = (cond_all.at[low, place], backs.at[place])[step]
        return pltpu.make_async_remote_copy(
            src, dst, high_send.at[step, h], high_recv.at[step, place],
            device_id={"dp": there * LOW + low}, device_id_type=MESH,
        )

    def low_copy(step, r, arriving):
        there = (low + r) % LOW
        place = there if arriving else low
        src = (cond_all.at[low], back.at[there])[step]
        dst = (cond_all.at[place], halves.at[place])[step]
        return pltpu.make_async_remote_copy(
            src, dst, low_send.at[step, r], low_recv.at[step, place],
            device_id={"dp": high * LOW + there}, device_id_type=MESH,
        )

    def scatter_copy(s):
        to = place_to(me, s)
        return pltpu.make_async_remote_copy(
            parcels.at[pl.ds(to * 2, 2)], partial.at[s], seq_send.at[0, s], seq_recv.at[0, s],
            device_id={"seq": to}, device_id_type=MESH,
        )

    def gather_copy(s, arriving):
        place = place_from(me, s) if arriving else me
        return pltpu.make_async_remote_copy(
            share, whole.at[pl.ds(place * 2, 2)], seq_send.at[1, s], seq_recv.at[1, s],
            device_id={"seq": place_to(me, s)}, device_id_type=MESH,
        )

    def each(low, high, action):
        pl.loop(low, high)(action)

    for a in range(4):
        fetch(a).start()
    for a in range(4):
        own_in(a).start()

    barrier = pltpu.get_barrier_semaphore()

    def signal(semaphore, **device):
        pl.semaphore_signal(semaphore, inc=1, device_id=device, device_id_type=MESH)

    def is_gateway(low, seq):
        return low == seq % LOW

    gateway = is_gateway(low, me)
    member = jnp.logical_not(gateway)

    @pl.loop(1, LOW)
    def _(r):
        there = (low + r) % LOW

        @pl.when(jnp.logical_not(is_gateway(there, me)))
        def _():
            signal(barrier, dp=high * LOW + there)

    @pl.loop(1, PEERS)
    def _(s):
        there = place_to(me, s)

        @pl.when(jnp.logical_not(is_gateway(low, there)))
        def _():
            signal(barrier, seq=there)

    cond_own[...] = jnp.zeros_like(cond_own)
    fetch(0).wait()
    cond_own[:, :weight_rows] = cond_ref[...]

    @pl.when(member)
    def _():
        pl.semaphore_wait(barrier, PEERS + LOW - 2)
        for there in range(0, PEERS, LOW):
            signal(entered, seq=low + there)
        signal(entered, dp=high * LOW + me % LOW)

    @pl.when(gateway)
    def _():
        pl.semaphore_wait(entered, PEERS - PEERS // LOW + LOW - 1)
        for h in range(1, HIGH):
            signal(barrier, dp=(high + h) % HIGH * LOW + low)


    each(1, PEERS, lambda s: inward(0, s).start())
    each(1, PEERS, lambda s: inward(1, s).start())

    def send_block(i):
        for s in range(max(i * BLOCK, 1), (i + 1) * BLOCK):
            inward(2, s).start()
            inward(3, s).start()

    send_block(0)
    cond_all[low, high] = cond_own[...]

    fetch(1).wait()
    fetch(2).wait()
    plain = jnp.zeros((8, features), jnp.float32)
    scaled = jnp.zeros((8, features), jnp.float32)
    for t in range(0, text_rows, 16):
        at = slice(t, t + 16)
        hidden = hidden_ref[at].astype(jnp.float32)
        incoming = incoming_ref[at].astype(jnp.float32)
        centred = hidden - jnp.sum(hidden, axis=-1, keepdims=True) * (1.0 / features)
        variance = jnp.sum(centred * centred, axis=-1, keepdims=True) * (1.0 / features)
        inv_std = lax.rsqrt(variance + NORM_EPS)
        norm = centred * inv_std
        normed[at] = norm
        spread[at] = jnp.broadcast_to(inv_std, (16, LANES))
        plain += jnp.sum(incoming.reshape(2, 8, features), axis=0)
        scaled += jnp.sum((incoming * norm).reshape(2, 8, features), axis=0)
    plain = jnp.sum(plain, axis=0, keepdims=True)
    scaled = jnp.sum(scaled, axis=0, keepdims=True)
    parcel[...] = jnp.zeros_like(parcel)
    back[...] = jnp.zeros_like(back)
    for p in range(SAMPLES):
        first = device_of(p) * columns
        at = slice(first, first + columns)
        parcel[p, :, LANES : LANES + columns] = plain[:, at]
        parcel[p, :, 2 * LANES : 2 * LANES + columns] = scaled[:, at]

    @pl.when(gateway)
    def _():
        pl.semaphore_wait(barrier, HIGH - 1)
        for r in range(1, LOW):
            signal(opened, dp=high * LOW + (low + r) % LOW)

    @pl.when(member)
    def _():
        pl.semaphore_wait(opened, 1)

    each(1, HIGH, lambda h: high_copy(0, h, False).start())
    each(1, HIGH, lambda h: high_copy(0, h, True).wait_recv())
    each(1, LOW, lambda r: low_copy(0, r, False).start())
    each(1, LOW, lambda r: low_copy(0, r, True).wait_recv())
    cond = cond_all[...].reshape(SAMPLES, cond_all.shape[3])[:, :weight_rows]
    act = (cond * jax.nn.sigmoid(cond)).astype(jnp.bfloat16)
    fetch(3).wait()
    parcel[:, :, :columns] = nn(act, weight_ref[1]).reshape(SAMPLES, 1, columns)
    each(1, SAMPLES, lambda r: dp_copy(r, False).start())

    def scatter_sums():
        parcels[rank_of(mine)] = parcel[rank_of(mine)]
        each(1, SAMPLES, lambda r: dp_copy(r, True).wait_recv())
        each(1, PEERS, lambda s: scatter_copy(s).start())

    def gather_sums():
        partial[0] = parcels[pl.ds(me * 2, 2)]
        each(1, PEERS, lambda s: scatter_copy(s).wait_recv())
        share[...] = jnp.sum(partial[...], axis=0)
        each(1, PEERS, lambda s: gather_copy(s, False).start())

    def weight_gradients():
        whole[pl.ds(me * 2, 2)] = share[...]
        each(1, PEERS, lambda s: gather_copy(s, True).wait_recv())
        sums = whole[...].reshape(SAMPLES, whole.shape[2])
        cond = cond_all[...].reshape(SAMPLES, cond_all.shape[3])[:, :weight_rows]
        act = (cond * jax.nn.sigmoid(cond)).astype(jnp.bfloat16).astype(jnp.float32)
        backward = jnp.zeros((SAMPLES, weight_rows), jnp.float32)
        for k in range(2):
            grad = sums[:, (k + 1) * LANES : (k + 1) * LANES + columns]
            weight_grad_ref[k] = lax.dot_general(
                act, grad, (((0,), (0,)), ((), ())),
                precision=lax.Precision.HIGHEST, preferred_element_type=jnp.float32,
            )
            backward += lax.dot_general(
                grad, weight_ref[k].astype(jnp.float32), (((1,), (1,)), ((), ())),
                precision=lax.Precision.HIGHEST, preferred_element_type=jnp.float32,
            )
        keep(0).start()
        back[:, :, :, :weight_rows] = backward.reshape(LOW, HIGH, 1, weight_rows)
        each(1, LOW, lambda r: low_copy(1, r, False).start())

    def half_sums():
        halves[low] = back[low]
        each(1, LOW, lambda r: low_copy(1, r, True).wait_recv())
        half[...] = jnp.sum(halves[...], axis=0)
        each(1, HIGH, lambda h: high_copy(1, h, False).start())

    def text_gradient():
        for j in range(SAMPLES):
            first = device_of(j) * columns
            row[:, first : first + columns] = whole[j, :, :columns]
        gain = 1.0 + row[...]
        for t in range(0, text_rows, 16):
            at = slice(t, t + 16)
            norm = normed[at]
            upstream = incoming_ref[at].astype(jnp.float32) * gain
            mean = jnp.sum(upstream, axis=-1, keepdims=True) * (1.0 / features)
            along = jnp.sum(upstream * norm, axis=-1, keepdims=True) * (1.0 / features)
            grad = spread[at, :1] * (upstream - mean - norm * along)
            hidden_grad_ref[at] = grad.astype(jnp.bfloat16)
        keep(1).start()

    def cond_gradient():
        backs[high] = half[high]
        each(1, HIGH, lambda h: high_copy(1, h, True).wait_recv())
        summed = jnp.sum(backs[...], axis=0)[:, :weight_rows]
        cond = cond_ref[...]
        sigma = jax.nn.sigmoid(cond)
        cond_grad_ref[...] = summed * sigma * (1.0 + cond * (1.0 - sigma))
        keep(2).start()

    dka[...] = jnp.zeros_like(dka)
    dva[...] = jnp.zeros_like(dva)
    for a in range(4):
        own_in(a).wait()
    each(1, PEERS, lambda s: inward(0, s).wait_recv())

    for s in range(PEERS):
        kt[:, s * rows : (s + 1) * rows] = kb[s].astype(jnp.float32).T.astype(jnp.bfloat16)

    send_block(1)
    each(1, PEERS, lambda s: inward(1, s).wait_recv())
    send_block(2)
    scatter_sums()

    per_chunk = CHUNK // rows

    @pl.loop(0, PEERS // BLOCK)
    def _(i):
        first = i * BLOCK
        for j in range(BLOCK):

            @pl.when(first + j > 0)
            def _():
                inward(2, first + j).wait_recv()
                inward(3, first + j).wait_recv()

        here = pl.ds(pl.multiple_of(first, BLOCK), BLOCK)
        queries = qb[here].reshape(block, width)
        grads = gb[here].reshape(block, width)
        peak = None
        for t in range(chunks):
            keys = kb[t * per_chunk : (t + 1) * per_chunk].reshape(CHUNK, width)
            scores = nt(keys, queries)
            u[t] = scores
            top = jnp.max(scores.reshape(CHUNK // 8, 8, block), axis=0)
            peak = top if peak is None else jnp.maximum(peak, top)
        peak = jnp.max(peak, axis=0, keepdims=True)
        total = jnp.zeros((8, block), jnp.float32)
        delta = jnp.zeros((8, block), jnp.float32)
        for t in range(chunks):
            values = vb[t * per_chunk : (t + 1) * per_chunk].reshape(CHUNK, width)
            prob_grad = nt(values, grads)
            exponent = jnp.exp2((u[t] - peak) * (factor * LOG2E))
            total += jnp.sum(exponent.reshape(CHUNK // 8, 8, block), axis=0)
            delta += jnp.sum((exponent * prob_grad).reshape(CHUNK // 8, 8, block), axis=0)
            u[t] = exponent
            dp[t] = prob_grad
        inverse = 1.0 / jnp.sum(total, axis=0, keepdims=True)
        delta = jnp.sum(delta, axis=0, keepdims=True) * inverse
        query_grad = jnp.zeros((width, block), jnp.float32)
        for t in range(chunks):
            at = slice(t * CHUNK, (t + 1) * CHUNK)
            probability = u[t] * inverse
            score_low = (probability * (dp[t] - delta)).astype(jnp.bfloat16)
            dva[at] += nn(probability.astype(jnp.bfloat16), grads)
            dka[at] += nn(score_low, queries)
            query_grad += nn(kt[:, at], score_low)
        dqo[here] = (
            (query_grad * factor).T.astype(jnp.bfloat16).reshape(BLOCK, rows, width)
        )
        for j in range(BLOCK):

            @pl.when(first + j > 0)
            def _():
                outward(0, first + j).start()

        @pl.when(i == 0)
        def _():
            send_block(3)
            gather_sums()

        pl.when(i == 1)(weight_gradients)
        pl.when(i == 2)(half_sums)

    own_out(0).start()
    for s in range(PEERS):
        at = slice(s * rows, (s + 1) * rows)
        dko[s] = (dka[at] * factor).astype(jnp.bfloat16)
        dvo[s] = dva[at].astype(jnp.bfloat16)

    @pl.loop(1, PEERS)
    def _(s):
        outward(1, s).start()
        outward(2, s).start()

    own_out(1).start()
    own_out(2).start()
    text_gradient()
    cond_gradient()

    @pl.loop(1, SAMPLES)
    def _(r):
        dp_copy(r, False).wait_send()

    for step in range(2):
        each(1, HIGH, lambda h: high_copy(step, h, False).wait_send())
        each(1, LOW, lambda r: low_copy(step, r, False).wait_send())

    @pl.loop(1, PEERS)
    def _(s):
        scatter_copy(s).wait_send()
        gather_copy(s, False).wait_send()

    @pl.loop(1, PEERS)
    def _(s):
        for a in range(4):
            inward(a, s).wait_send()
        for a in range(3):
            outward(a, s).wait_send()

    for a in range(3):
        own_out(a).wait()
        keep(a).wait()

    @pl.loop(1, PEERS)
    def _(s):
        for a in range(3):
            outward(a, s).wait_recv()


def joint(cond, weight, hidden, incoming, q, k, v, g):
    rows, width = q.shape
    slots = pltpu.VMEM((PEERS, rows, HEAD_DIM), jnp.bfloat16)
    tokens = PEERS * rows
    scores = pltpu.VMEM((tokens // CHUNK, CHUNK, BLOCK * rows), jnp.float32)
    total = pltpu.VMEM((tokens, HEAD_DIM), jnp.float32)
    anywhere = pl.BlockSpec(memory_space=pl.ANY)
    padded = -(-cond.shape[1] // LANES) * LANES
    f32 = jnp.float32
    return pl.pallas_call(
        joint_kernel,
        out_shape=[
            jax.ShapeDtypeStruct(hidden.shape, jnp.bfloat16),
            jax.ShapeDtypeStruct(weight.shape, f32),
            jax.ShapeDtypeStruct(cond.shape, f32),
        ]
        + [jax.ShapeDtypeStruct((rows, width), jnp.bfloat16)] * 3,
        in_specs=[anywhere] * 8,
        out_specs=[anywhere] * 6,
        scratch_shapes=[
            pltpu.VMEM(cond.shape, f32),
            pltpu.VMEM(weight.shape, jnp.bfloat16),
            pltpu.VMEM(hidden.shape, jnp.bfloat16),
            pltpu.VMEM(hidden.shape, jnp.bfloat16),
            pltpu.VMEM(hidden.shape, jnp.bfloat16),
            pltpu.VMEM(weight.shape, f32),
            pltpu.VMEM(cond.shape, f32),
            slots, slots, slots, slots,
            pltpu.VMEM((HEAD_DIM, tokens), jnp.bfloat16),
            scores, scores, total, total,
            slots, slots, slots,
            pltpu.VMEM((1, padded), f32),
            pltpu.VMEM((LOW, HIGH, 1, padded), f32),
            pltpu.VMEM((SAMPLES, 1, 3 * LANES), f32),
            pltpu.VMEM((SAMPLES, 1, 3 * LANES), f32),
            pltpu.VMEM((PEERS, 2, 1, 3 * LANES), f32),
            pltpu.VMEM((2, 1, 3 * LANES), f32),
            pltpu.VMEM((SAMPLES, 1, 3 * LANES), f32),
            pltpu.VMEM((LOW, HIGH, 1, padded), f32),
            pltpu.VMEM((LOW, HIGH, 1, padded), f32),
            pltpu.VMEM((HIGH, 1, padded), f32),
            pltpu.VMEM((HIGH, 1, padded), f32),
            pltpu.VMEM((1, hidden.shape[1]), f32),
            pltpu.VMEM(hidden.shape, f32),
            pltpu.VMEM((hidden.shape[0], LANES), f32),
            pltpu.SemaphoreType.DMA((7, PEERS)),
            pltpu.SemaphoreType.DMA((7, PEERS)),
            pltpu.SemaphoreType.DMA((14,)),
            pltpu.SemaphoreType.DMA((SAMPLES,)),
            pltpu.SemaphoreType.DMA((SAMPLES,)),
            pltpu.SemaphoreType.DMA((2, LOW)),
            pltpu.SemaphoreType.DMA((2, LOW)),
            pltpu.SemaphoreType.DMA((2, HIGH)),
            pltpu.SemaphoreType.DMA((2, HIGH)),
            pltpu.SemaphoreType.DMA((2, PEERS)),
            pltpu.SemaphoreType.DMA((2, PEERS)),
            pltpu.SemaphoreType.REGULAR,
            pltpu.SemaphoreType.REGULAR,
        ],
        compiler_params=pltpu.CompilerParams(
            collective_id=0, has_side_effects=True, vmem_limit_bytes=62 * 2**20
        ),
        cost_estimate=pl.CostEstimate(
            flops=10 * tokens * tokens * HEAD_DIM,
            bytes_accessed=14 * rows * width,
            transcendentals=tokens * tokens,
        ),
    )(cond, weight, hidden, incoming, q, k, v, g)


def deliver_kernel(*refs):
    count = (len(refs) - 2) // 3
    sources, results, passing = refs[:count], refs[count : 2 * count], refs[2 * count : 3 * count]
    arrived, done = refs[3 * count :]
    loads = [pltpu.make_async_copy(sources[n], passing[n], arrived.at[n]) for n in range(count)]
    stores = [pltpu.make_async_copy(passing[n], results[n], done.at[n]) for n in range(count)]
    for load in loads:
        load.start()
    for load, store in zip(loads, stores):
        load.wait()
        store.start()
    for store in stores:
        store.wait()


def deliver(results):
    anywhere = pl.BlockSpec(memory_space=pl.ANY)
    return pl.pallas_call(
        deliver_kernel,
        out_shape=[jax.ShapeDtypeStruct(r.shape, r.dtype) for r in results],
        in_specs=[anywhere] * len(results),
        out_specs=[anywhere] * len(results),
        scratch_shapes=[pltpu.VMEM(r.shape, r.dtype) for r in results]
        + [pltpu.SemaphoreType.DMA((len(results),))] * 2,
        compiler_params=pltpu.CompilerParams(vmem_limit_bytes=62 * 2**20),
    )(*results)


def per_device(cond_vec, mod_weight, text_hidden, text_grad, queries, keys, values, out_grad):
    grads = joint(
        cond_vec, mod_weight, text_hidden[0], text_grad[0],
        queries[0], keys[0], values[0], out_grad[0],
    )
    grads = deliver(grads)
    hidden_grad, weight_grad, cond_grad, query_grad, key_grad, value_grad = grads
    return (
        hidden_grad[None], weight_grad, cond_grad,
        query_grad[None], key_grad[None], value_grad[None],
    )


def solution(mesh):
    tokens = P("dp", "seq", None)
    weights = P(None, "seq", "dp")
    return jax.shard_map(
        per_device,
        mesh=mesh,
        in_specs=(P("dp", "seq"), weights, tokens, tokens, tokens, tokens, tokens, tokens),
        out_specs=(tokens, weights, P("dp", "seq"), tokens, tokens, tokens),
        check_vma=False,
    )
```

```python
import math

import jax
import jax.numpy as jnp
from jax import lax
from jax.experimental import pallas as pl
from jax.experimental.pallas import tpu as pltpu
from jax.sharding import PartitionSpec as P

HEADS = 16
HEAD_DIM = 128
NORM_EPS = 1e-06
PEERS = 16
SAMPLES = 32
LANES = 128
HIGH, LOW = 4, 8
BLOCK = 4
CHUNK = 256
LOG2E = math.log2(math.e)
MESH = pl.DeviceIdType.MESH


def place_to(me, s):
    return ((me // 4 + s % 4) % 4) * 4 + (me % 4 + s // 4) % 4


def place_from(me, s):
    return ((me // 4 + 4 - s % 4) % 4) * 4 + (me % 4 + 4 - s // 4) % 4


def rank_of(device):
    return device % LOW * HIGH + device // LOW


def device_of(rank):
    return rank % HIGH * LOW + rank // HIGH


def nt(a, b):
    return lax.dot_general(a, b, (((1,), (1,)), ((), ())), preferred_element_type=jnp.float32)


def nn(a, b):
    return lax.dot_general(a, b, (((1,), (0,)), ((), ())), preferred_element_type=jnp.float32)


def joint_kernel(
    cond_in, weight_in, hidden_in, incoming_in, q_ref, k_ref, v_ref, g_ref,
    hidden_grad_out, weight_grad_out, cond_grad_out, dq_ref, dk_ref, dv_ref,
    cond_ref, weight_ref, hidden_ref, incoming_ref, hidden_grad_ref, weight_grad_ref, cond_grad_ref,
    qb, kb, vb, gb, kt, u, dp, dka, dva, dqo, dko, dvo,
    cond_own, cond_all, parcel, parcels, partial, share, whole, back, halves, half, backs,
    row, normed, spread,
    send, recv, local, dp_send, dp_recv, low_send, low_recv, high_send, high_recv,
    seq_send, seq_recv, entered, opened,
):
    rows = q_ref.shape[0]
    width = qb.shape[2]
    tokens = PEERS * rows
    chunks = tokens // CHUNK
    block = BLOCK * rows
    factor = width ** (-0.5)
    me = lax.axis_index("seq")
    mine = lax.axis_index("dp")
    low, high = mine % LOW, mine // LOW
    weight_rows, columns = weight_ref.shape[1:]
    features = hidden_ref.shape[1]
    text_rows = hidden_ref.shape[0]

    def head_of(device):
        return pl.ds(pl.multiple_of(device * width, width), width)

    ins = ((k_ref, kb), (v_ref, vb), (q_ref, qb), (g_ref, gb))
    outs = ((dqo, dq_ref), (dko, dk_ref), (dvo, dv_ref))

    def inward(a, s):
        src, dst = ins[a]
        to = place_to(me, s)
        return pltpu.make_async_remote_copy(
            src.at[:, head_of(to)], dst.at[s], send.at[a, s], recv.at[a, s],
            device_id={"seq": to}, device_id_type=MESH,
        )

    def outward(a, s):
        src, dst = outs[a]
        return pltpu.make_async_remote_copy(
            src.at[s], dst.at[:, head_of(me)], send.at[4 + a, s], recv.at[4 + a, s],
            device_id={"seq": place_from(me, s)}, device_id_type=MESH,
        )

    def own_in(a):
        src, dst = ins[a]
        return pltpu.make_async_copy(src.at[:, head_of(me)], dst.at[0], local.at[a])

    def own_out(a):
        src, dst = outs[a]
        return pltpu.make_async_copy(src.at[0], dst.at[:, head_of(me)], local.at[4 + a])

    fetched = ((cond_in, cond_ref), (hidden_in, hidden_ref), (incoming_in, incoming_ref),
               (weight_in, weight_ref))
    kept = ((weight_grad_ref, weight_grad_out), (hidden_grad_ref, hidden_grad_out),
            (cond_grad_ref, cond_grad_out))

    def fetch(a):
        return pltpu.make_async_copy(*fetched[a], local.at[7 + a])

    def keep(a):
        return pltpu.make_async_copy(*kept[a], local.at[11 + a])

    def other(r):
        return (mine + r) % SAMPLES

    def dp_copy(r, arriving):
        there = rank_of(other(r))
        place = there if arriving else rank_of(mine)
        return pltpu.make_async_remote_copy(
            parcel.at[there], parcels.at[place], dp_send.at[r], dp_recv.at[place],
            device_id={"dp": other(r)}, device_id_type=MESH,
        )

    def high_copy(step, h, arriving):
        there = (high + h) % HIGH
        place = there if arriving else high
        src = (cond_own, half.at[there])[step]
        dst = (cond_all.at[low, place], backs.at[place])[step]
        return pltpu.make_async_remote_copy(
            src, dst, high_send.at[step, h], high_recv.at[step, place],
            device_id={"dp": there * LOW + low}, device_id_type=MESH,
        )

    def low_copy(step, r, arriving):
        there = (low + r) % LOW
        place = there if arriving else low
        src = (cond_all.at[low], back.at[there])[step]
        dst = (cond_all.at[place], halves.at[place])[step]
        return pltpu.make_async_remote_copy(
            src, dst, low_send.at[step, r], low_recv.at[step, place],
            device_id={"dp": high * LOW + there}, device_id_type=MESH,
        )

    def scatter_copy(s):
        to = place_to(me, s)
        return pltpu.make_async_remote_copy(
            parcels.at[pl.ds(to * 2, 2)], partial.at[s], seq_send.at[0, s], seq_recv.at[0, s],
            device_id={"seq": to}, device_id_type=MESH,
        )

    def gather_copy(s, arriving):
        place = place_from(me, s) if arriving else me
        return pltpu.make_async_remote_copy(
            share, whole.at[pl.ds(place * 2, 2)], seq_send.at[1, s], seq_recv.at[1, s],
            device_id={"seq": place_to(me, s)}, device_id_type=MESH,
        )

    def each(low, high, action):
        pl.loop(low, high)(action)

    for a in range(4):
        fetch(a).start()
    for a in range(4):
        own_in(a).start()

    barrier = pltpu.get_barrier_semaphore()

    def signal(semaphore, **device):
        pl.semaphore_signal(semaphore, inc=1, device_id=device, device_id_type=MESH)

    def is_gateway(low, seq):
        return low == seq % LOW

    gateway = is_gateway(low, me)
    member = jnp.logical_not(gateway)

    @pl.loop(1, LOW)
    def _(r):
        there = (low + r) % LOW

        @pl.when(jnp.logical_not(is_gateway(there, me)))
        def _():
            signal(barrier, dp=high * LOW + there)

    @pl.loop(1, PEERS)
    def _(s):
        there = place_to(me, s)

        @pl.when(jnp.logical_not(is_gateway(low, there)))
        def _():
            signal(barrier, seq=there)

    cond_own[...] = jnp.zeros_like(cond_own)
    fetch(0).wait()
    cond_own[:, :weight_rows] = cond_ref[...]

    @pl.when(member)
    def _():
        pl.semaphore_wait(barrier, PEERS + LOW - 2)
        for there in range(0, PEERS, LOW):
            signal(entered, seq=low + there)
        signal(entered, dp=high * LOW + me % LOW)

    @pl.when(gateway)
    def _():
        pl.semaphore_wait(entered, PEERS - PEERS // LOW + LOW - 1)
        for h in range(1, HIGH):
            signal(barrier, dp=(high + h) % HIGH * LOW + low)


    each(1, PEERS, lambda s: inward(0, s).start())

    def send_block(i):
        for s in range(max(i * BLOCK, 1), (i + 1) * BLOCK):
            inward(2, s).start()
            inward(3, s).start()

    cond_all[low, high] = cond_own[...]

    fetch(1).wait()
    fetch(2).wait()
    plain = jnp.zeros((8, features), jnp.float32)
    scaled = jnp.zeros((8, features), jnp.float32)
    for t in range(0, text_rows, 16):
        at = slice(t, t + 16)
        hidden = hidden_ref[at].astype(jnp.float32)
        incoming = incoming_ref[at].astype(jnp.float32)
        centred = hidden - jnp.sum(hidden, axis=-1, keepdims=True) * (1.0 / features)
        variance = jnp.sum(centred * centred, axis=-1, keepdims=True) * (1.0 / features)
        inv_std = lax.rsqrt(variance + NORM_EPS)
        norm = centred * inv_std
        normed[at] = norm
        spread[at] = jnp.broadcast_to(inv_std, (16, LANES))
        plain += jnp.sum(incoming.reshape(2, 8, features), axis=0)
        scaled += jnp.sum((incoming * norm).reshape(2, 8, features), axis=0)
    plain = jnp.sum(plain, axis=0, keepdims=True)
    scaled = jnp.sum(scaled, axis=0, keepdims=True)
    parcel[...] = jnp.zeros_like(parcel)
    back[...] = jnp.zeros_like(back)
    for p in range(SAMPLES):
        first = device_of(p) * columns
        at = slice(first, first + columns)
        parcel[p, :, LANES : LANES + columns] = plain[:, at]
        parcel[p, :, 2 * LANES : 2 * LANES + columns] = scaled[:, at]

    @pl.when(gateway)
    def _():
        pl.semaphore_wait(barrier, HIGH - 1)
        for r in range(1, LOW):
            signal(opened, dp=high * LOW + (low + r) % LOW)

    @pl.when(member)
    def _():
        pl.semaphore_wait(opened, 1)

    each(1, HIGH, lambda h: high_copy(0, h, False).start())
    each(1, PEERS, lambda s: inward(1, s).start())
    send_block(0)
    each(1, HIGH, lambda h: high_copy(0, h, True).wait_recv())
    each(1, LOW, lambda r: low_copy(0, r, False).start())
    send_block(1)
    each(1, LOW, lambda r: low_copy(0, r, True).wait_recv())
    cond = cond_all[...].reshape(SAMPLES, cond_all.shape[3])[:, :weight_rows]
    act = (cond * jax.nn.sigmoid(cond)).astype(jnp.bfloat16)
    fetch(3).wait()
    parcel[:, :, :columns] = nn(act, weight_ref[1]).reshape(SAMPLES, 1, columns)
    each(1, SAMPLES, lambda r: dp_copy(r, False).start())
    send_block(2)

    def scatter_sums():
        parcels[rank_of(mine)] = parcel[rank_of(mine)]
        each(1, SAMPLES, lambda r: dp_copy(r, True).wait_recv())
        each(1, PEERS, lambda s: scatter_copy(s).start())

    def gather_sums():
        partial[0] = parcels[pl.ds(me * 2, 2)]
        each(1, PEERS, lambda s: scatter_copy(s).wait_recv())
        share[...] = jnp.sum(partial[...], axis=0)
        each(1, PEERS, lambda s: gather_copy(s, False).start())

    def weight_gradients():
        whole[pl.ds(me * 2, 2)] = share[...]
        each(1, PEERS, lambda s: gather_copy(s, True).wait_recv())
        sums = whole[...].reshape(SAMPLES, whole.shape[2])
        cond = cond_all[...].reshape(SAMPLES, cond_all.shape[3])[:, :weight_rows]
        act = (cond * jax.nn.sigmoid(cond)).astype(jnp.bfloat16).astype(jnp.float32)
        backward = jnp.zeros((SAMPLES, weight_rows), jnp.float32)
        for k in range(2):
            grad = sums[:, (k + 1) * LANES : (k + 1) * LANES + columns]
            weight_grad_ref[k] = lax.dot_general(
                act, grad, (((0,), (0,)), ((), ())),
                precision=lax.Precision.HIGHEST, preferred_element_type=jnp.float32,
            )
            backward += lax.dot_general(
                grad, weight_ref[k].astype(jnp.float32), (((1,), (1,)), ((), ())),
                precision=lax.Precision.HIGHEST, preferred_element_type=jnp.float32,
            )
        keep(0).start()
        back[:, :, :, :weight_rows] = backward.reshape(LOW, HIGH, 1, weight_rows)
        each(1, LOW, lambda r: low_copy(1, r, False).start())

    def half_sums():
        halves[low] = back[low]
        each(1, LOW, lambda r: low_copy(1, r, True).wait_recv())
        half[...] = jnp.sum(halves[...], axis=0)
        each(1, HIGH, lambda h: high_copy(1, h, False).start())

    def text_gradient():
        for j in range(SAMPLES):
            first = device_of(j) * columns
            row[:, first : first + columns] = whole[j, :, :columns]
        gain = 1.0 + row[...]
        for t in range(0, text_rows, 16):
            at = slice(t, t + 16)
            norm = normed[at]
            upstream = incoming_ref[at].astype(jnp.float32) * gain
            mean = jnp.sum(upstream, axis=-1, keepdims=True) * (1.0 / features)
            along = jnp.sum(upstream * norm, axis=-1, keepdims=True) * (1.0 / features)
            grad = spread[at, :1] * (upstream - mean - norm * along)
            hidden_grad_ref[at] = grad.astype(jnp.bfloat16)
        keep(1).start()

    def cond_gradient():
        backs[high] = half[high]
        each(1, HIGH, lambda h: high_copy(1, h, True).wait_recv())
        summed = jnp.sum(backs[...], axis=0)[:, :weight_rows]
        cond = cond_ref[...]
        sigma = jax.nn.sigmoid(cond)
        cond_grad_ref[...] = summed * sigma * (1.0 + cond * (1.0 - sigma))
        keep(2).start()

    dka[...] = jnp.zeros_like(dka)
    dva[...] = jnp.zeros_like(dva)
    for a in range(4):
        own_in(a).wait()
    each(1, PEERS, lambda s: inward(0, s).wait_recv())

    for s in range(PEERS):
        kt[:, s * rows : (s + 1) * rows] = kb[s].astype(jnp.float32).T.astype(jnp.bfloat16)

    each(1, PEERS, lambda s: inward(1, s).wait_recv())

    per_chunk = CHUNK // rows

    @pl.loop(0, PEERS // BLOCK)
    def _(i):
        first = i * BLOCK
        for j in range(BLOCK):

            @pl.when(first + j > 0)
            def _():
                inward(2, first + j).wait_recv()
                inward(3, first + j).wait_recv()

        here = pl.ds(pl.multiple_of(first, BLOCK), BLOCK)
        queries = qb[here].reshape(block, width)
        grads = gb[here].reshape(block, width)
        peak = None
        for t in range(chunks):
            keys = kb[t * per_chunk : (t + 1) * per_chunk].reshape(CHUNK, width)
            scores = nt(keys, queries)
            u[t] = scores
            top = jnp.max(scores.reshape(CHUNK // 8, 8, block), axis=0)
            peak = top if peak is None else jnp.maximum(peak, top)
        peak = jnp.max(peak, axis=0, keepdims=True)
        total = jnp.zeros((8, block), jnp.float32)
        delta = jnp.zeros((8, block), jnp.float32)
        for t in range(chunks):
            values = vb[t * per_chunk : (t + 1) * per_chunk].reshape(CHUNK, width)
            prob_grad = nt(values, grads)
            exponent = jnp.exp2((u[t] - peak) * (factor * LOG2E))
            total += jnp.sum(exponent.reshape(CHUNK // 8, 8, block), axis=0)
            delta += jnp.sum((exponent * prob_grad).reshape(CHUNK // 8, 8, block), axis=0)
            u[t] = exponent
            dp[t] = prob_grad
        inverse = 1.0 / jnp.sum(total, axis=0, keepdims=True)
        delta = jnp.sum(delta, axis=0, keepdims=True) * inverse
        query_grad = jnp.zeros((width, block), jnp.float32)
        for t in range(chunks):
            at = slice(t * CHUNK, (t + 1) * CHUNK)
            probability = u[t] * inverse
            score_low = (probability * (dp[t] - delta)).astype(jnp.bfloat16)
            dva[at] += nn(probability.astype(jnp.bfloat16), grads)
            dka[at] += nn(score_low, queries)
            query_grad += nn(kt[:, at], score_low)
        dqo[here] = (
            (query_grad * factor).T.astype(jnp.bfloat16).reshape(BLOCK, rows, width)
        )
        for j in range(BLOCK):

            @pl.when(first + j > 0)
            def _():
                outward(0, first + j).start()

        @pl.when(i == 0)
        def _():
            send_block(3)

        pl.when(i == 1)(scatter_sums)
        pl.when(i == 2)(gather_sums)
        pl.when(i == 3)(weight_gradients)

    own_out(0).start()
    for s in range(PEERS):
        at = slice(s * rows, (s + 1) * rows)
        dko[s] = (dka[at] * factor).astype(jnp.bfloat16)
    each(1, PEERS, lambda s: outward(1, s).start())
    own_out(1).start()
    half_sums()
    for s in range(PEERS):
        at = slice(s * rows, (s + 1) * rows)
        dvo[s] = dva[at].astype(jnp.bfloat16)
    each(1, PEERS, lambda s: outward(2, s).start())
    own_out(2).start()
    text_gradient()
    cond_gradient()

    @pl.loop(1, SAMPLES)
    def _(r):
        dp_copy(r, False).wait_send()

    for step in range(2):
        each(1, HIGH, lambda h: high_copy(step, h, False).wait_send())
        each(1, LOW, lambda r: low_copy(step, r, False).wait_send())

    @pl.loop(1, PEERS)
    def _(s):
        scatter_copy(s).wait_send()
        gather_copy(s, False).wait_send()

    @pl.loop(1, PEERS)
    def _(s):
        for a in range(4):
            inward(a, s).wait_send()
        for a in range(3):
            outward(a, s).wait_send()

    for a in range(3):
        own_out(a).wait()
        keep(a).wait()

    @pl.loop(1, PEERS)
    def _(s):
        for a in range(3):
            outward(a, s).wait_recv()


def joint(cond, weight, hidden, incoming, q, k, v, g):
    rows, width = q.shape
    slots = pltpu.VMEM((PEERS, rows, HEAD_DIM), jnp.bfloat16)
    tokens = PEERS * rows
    scores = pltpu.VMEM((tokens // CHUNK, CHUNK, BLOCK * rows), jnp.float32)
    total = pltpu.VMEM((tokens, HEAD_DIM), jnp.float32)
    anywhere = pl.BlockSpec(memory_space=pl.ANY)
    padded = -(-cond.shape[1] // LANES) * LANES
    f32 = jnp.float32
    return pl.pallas_call(
        joint_kernel,
        out_shape=[
            jax.ShapeDtypeStruct(hidden.shape, jnp.bfloat16),
            jax.ShapeDtypeStruct(weight.shape, f32),
            jax.ShapeDtypeStruct(cond.shape, f32),
        ]
        + [jax.ShapeDtypeStruct((rows, width), jnp.bfloat16)] * 3,
        in_specs=[anywhere] * 8,
        out_specs=[anywhere] * 6,
        scratch_shapes=[
            pltpu.VMEM(cond.shape, f32),
            pltpu.VMEM(weight.shape, jnp.bfloat16),
            pltpu.VMEM(hidden.shape, jnp.bfloat16),
            pltpu.VMEM(hidden.shape, jnp.bfloat16),
            pltpu.VMEM(hidden.shape, jnp.bfloat16),
            pltpu.VMEM(weight.shape, f32),
            pltpu.VMEM(cond.shape, f32),
            slots, slots, slots, slots,
            pltpu.VMEM((HEAD_DIM, tokens), jnp.bfloat16),
            scores, scores, total, total,
            slots, slots, slots,
            pltpu.VMEM((1, padded), f32),
            pltpu.VMEM((LOW, HIGH, 1, padded), f32),
            pltpu.VMEM((SAMPLES, 1, 3 * LANES), f32),
            pltpu.VMEM((SAMPLES, 1, 3 * LANES), f32),
            pltpu.VMEM((PEERS, 2, 1, 3 * LANES), f32),
            pltpu.VMEM((2, 1, 3 * LANES), f32),
            pltpu.VMEM((SAMPLES, 1, 3 * LANES), f32),
            pltpu.VMEM((LOW, HIGH, 1, padded), f32),
            pltpu.VMEM((LOW, HIGH, 1, padded), f32),
            pltpu.VMEM((HIGH, 1, padded), f32),
            pltpu.VMEM((HIGH, 1, padded), f32),
            pltpu.VMEM((1, hidden.shape[1]), f32),
            pltpu.VMEM(hidden.shape, f32),
            pltpu.VMEM((hidden.shape[0], LANES), f32),
            pltpu.SemaphoreType.DMA((7, PEERS)),
            pltpu.SemaphoreType.DMA((7, PEERS)),
            pltpu.SemaphoreType.DMA((14,)),
            pltpu.SemaphoreType.DMA((SAMPLES,)),
            pltpu.SemaphoreType.DMA((SAMPLES,)),
            pltpu.SemaphoreType.DMA((2, LOW)),
            pltpu.SemaphoreType.DMA((2, LOW)),
            pltpu.SemaphoreType.DMA((2, HIGH)),
            pltpu.SemaphoreType.DMA((2, HIGH)),
            pltpu.SemaphoreType.DMA((2, PEERS)),
            pltpu.SemaphoreType.DMA((2, PEERS)),
            pltpu.SemaphoreType.REGULAR,
            pltpu.SemaphoreType.REGULAR,
        ],
        compiler_params=pltpu.CompilerParams(
            collective_id=0, has_side_effects=True, vmem_limit_bytes=62 * 2**20
        ),
        cost_estimate=pl.CostEstimate(
            flops=10 * tokens * tokens * HEAD_DIM,
            bytes_accessed=14 * rows * width,
            transcendentals=tokens * tokens,
        ),
    )(cond, weight, hidden, incoming, q, k, v, g)


def deliver_kernel(*refs):
    count = (len(refs) - 2) // 3
    sources, results, passing = refs[:count], refs[count : 2 * count], refs[2 * count : 3 * count]
    arrived, done = refs[3 * count :]
    loads = [pltpu.make_async_copy(sources[n], passing[n], arrived.at[n]) for n in range(count)]
    stores = [pltpu.make_async_copy(passing[n], results[n], done.at[n]) for n in range(count)]
    for load in loads:
        load.start()
    for load, store in zip(loads, stores):
        load.wait()
        store.start()
    for store in stores:
        store.wait()


def deliver(results):
    anywhere = pl.BlockSpec(memory_space=pl.ANY)
    return pl.pallas_call(
        deliver_kernel,
        out_shape=[jax.ShapeDtypeStruct(r.shape, r.dtype) for r in results],
        in_specs=[anywhere] * len(results),
        out_specs=[anywhere] * len(results),
        scratch_shapes=[pltpu.VMEM(r.shape, r.dtype) for r in results]
        + [pltpu.SemaphoreType.DMA((len(results),))] * 2,
        compiler_params=pltpu.CompilerParams(vmem_limit_bytes=62 * 2**20),
    )(*results)


def per_device(cond_vec, mod_weight, text_hidden, text_grad, queries, keys, values, out_grad):
    grads = joint(
        cond_vec, mod_weight, text_hidden[0], text_grad[0],
        queries[0], keys[0], values[0], out_grad[0],
    )
    grads = deliver(grads)
    hidden_grad, weight_grad, cond_grad, query_grad, key_grad, value_grad = grads
    return (
        hidden_grad[None], weight_grad, cond_grad,
        query_grad[None], key_grad[None], value_grad[None],
    )


def solution(mesh):
    tokens = P("dp", "seq", None)
    weights = P(None, "seq", "dp")
    return jax.shard_map(
        per_device,
        mesh=mesh,
        in_specs=(P("dp", "seq"), weights, tokens, tokens, tokens, tokens, tokens, tokens),
        out_specs=(tokens, weights, P("dp", "seq"), tokens, tokens, tokens),
        check_vma=False,
    )
```
